128 devices in a mesh: rows: 32 (over y, z, x_lo), cols: 4 (over x_hi, core).
Axes of the slice: x: 4 (x_hi: 2, x_lo: 2; x = x_hi * 2 + x_lo), y: 4, z: 4, core: 2. Of those that a mesh axis runs over, the one named last changes fastest.
Arguments:
- image: bfloat16 [1024, 192, 512], P('rows', None, 'cols'), may hold values from -6 to 6
- w_expand: bfloat16 [192, 768], replicated, may hold values from -0.4375 to 0.4375
- dw_kernel: bfloat16 [3, 3, 768], replicated, may hold values from -2 to 2
- w_project: bfloat16 [192, 768], replicated, may hold values from -0.21875 to 0.21875
- block_qkv: bfloat16 [192, 576], replicated, may hold values from -2 to 2
- block_out: bfloat16 [192, 192], replicated, may hold values from -0.4375 to 0.4375
- block_bias: float32 [6, 15, 15], replicated, may hold values from -4 to 4
- mlp_in: bfloat16 [192, 768], replicated, may hold values from -0.4375 to 0.4375
- mlp_out: bfloat16 [192, 768], replicated, may hold values from -0.21875 to 0.21875
- grid_qkv: bfloat16 [192, 576], replicated, may hold values from -2 to 2
- grid_out: bfloat16 [192, 192], replicated, may hold values from -0.4375 to 0.4375
- grid_bias: float32 [6, 15, 15], replicated, may hold values from -4 to 4
- mlp2_in: bfloat16 [192, 768], replicated, may hold values from -0.4375 to 0.4375
- mlp2_out: bfloat16 [192, 768], replicated, may hold values from -0.21875 to 0.21875
Outputs:
- result: bfloat16 [1024, 192, 512], P('rows', None, 'cols')
The draws below stay inside these ranges and needn't reach their ends.
All inputs are finite; a program needn't handle non-finite values.
Results may differ from the reference program's by a relative error of at most 0.03.
Values may be sent and summed in bfloat16 or wider, within the bound.
No kernel may reach another device: no remote copies, remote signals or barrier semaphores. Data moves between devices by JAX's collectives and lax.ppermute only.
A program may use at most 128 MiB of HBM per device.

```python
import math
import jax
import jax.numpy as jnp
from jax import lax

ROWS_DEV = 32
COLS_DEV = 128
HEADS = 6
HEAD_DIM = 32
HID = 768
WIN = 8
D = 192
HEIGHT = 1024
WIDTH = 512
N_ROWS = 32
N_COLS = 4


def projection_weights(key, top):
    first, second = jax.random.split(key, 2)
    base = jax.random.normal(first, (D, 3 * D), jnp.float32) * D ** (-0.5)
    lift = jnp.exp(jax.random.uniform(second, (HEADS,), jnp.float32) * math.log(top))
    lift = jnp.repeat(lift, HEAD_DIM)
    query = base[:, :D] * lift
    keys = base[:, D:2 * D] * lift
    values = base[:, 2 * D:]
    return jnp.clip(jnp.concatenate([query, keys, values], axis=1), -2.0, 2.0)


def draw_block_qkv(key, part):
    key = jax.random.fold_in(key, 11)
    return projection_weights(key, 1.0).astype(jnp.bfloat16)


def draw_grid_qkv(key, part):
    key = jax.random.fold_in(key, 23)
    return projection_weights(key, 1.0).astype(jnp.bfloat16)


def block_scale(key, dims, shards, smallest, high):
    def one(dim, shards_of):
        steps = jax.random.uniform(jax.random.fold_in(jax.random.fold_in(key, 6), dim), (shards_of,), jnp.float32, smallest / len(shards), high / len(shards))
        return jnp.repeat(jnp.exp(steps), dims[dim] // shards_of).reshape((-1,) + (1,) * (len(dims) - dim - 1))

    level = one(*shards[0])
    for cut in shards[1:]:
        level = level * one(*cut)
    return level


def scatter_about(rng, shape, deviation, bound, pieces=(), kind=jnp.bfloat16):
    entries = deviation * jax.random.normal(rng, shape, jnp.float32)
    if pieces:
        entries = entries * block_scale(rng, shape, pieces, -0.22, 0.18)
    return jnp.clip(entries, -bound, bound).astype(kind)


def setup_inputs(seed: int = 0) -> dict:
    key_list = jax.random.split(jax.random.key(seed), 15)
    image = scatter_about(key_list[0], (HEIGHT, D, WIDTH), 1.0, 6.0, ((0, 32), (2, 4)))
    w_expand = scatter_about(key_list[1], (D, HID), D ** -0.5, 0.4375)
    dw_kernel = scatter_about(key_list[2], (3, 3, HID), 9 ** -0.5, 2.0)
    w_project = scatter_about(key_list[3], (D, HID), HID ** -0.5, 0.21875)
    block_qkv = draw_block_qkv(jax.random.fold_in(key_list[14], 71), 0)
    block_out = scatter_about(key_list[5], (D, D), D ** -0.5, 0.4375)
    block_bias = scatter_about(key_list[6], (HEADS, 2 * WIN - 1, 2 * WIN - 1), 1.0, 4.0, (), jnp.float32)
    mlp_in = scatter_about(key_list[7], (D, HID), D ** -0.5, 0.4375)
    mlp_out = scatter_about(key_list[8], (D, HID), HID ** -0.5, 0.21875)
    grid_qkv = draw_grid_qkv(jax.random.fold_in(key_list[14], 71), 0)
    grid_out = scatter_about(key_list[10], (D, D), D ** -0.5, 0.4375)
    grid_bias = scatter_about(key_list[11], (HEADS, 2 * WIN - 1, 2 * WIN - 1), 1.0, 4.0, (), jnp.float32)
    mlp2_in = scatter_about(key_list[12], (D, HID), D ** -0.5, 0.4375)
    mlp2_out = scatter_about(key_list[13], (D, HID), HID ** -0.5, 0.21875)
    return {"image": image, "w_expand": w_expand, "dw_kernel": dw_kernel, "w_project": w_project, "block_qkv": block_qkv, "block_out": block_out, "block_bias": block_bias, "mlp_in": mlp_in, "mlp_out": mlp_out, "grid_qkv": grid_qkv, "grid_out": grid_out, "grid_bias": grid_bias, "mlp2_in": mlp2_in, "mlp2_out": mlp2_out}


def normalize(tokens):
    values = tokens.astype(jnp.float32)
    centre = values - lax.optimization_barrier(jnp.mean(values, axis=-1, keepdims=True))
    spread = lax.optimization_barrier(jnp.mean(centre * centre, axis=-1, keepdims=True))
    return (centre * lax.rsqrt(spread + 1e-05)).astype(jnp.bfloat16)

def relative_bias(table):
    span = table.shape[1]
    side = (span + 1) // 2
    place = jnp.arange(side * side, dtype=jnp.int32)
    row_of = place // side
    col_of = place % side
    index = (row_of[:, None] - row_of[None, :] + side - 1) * span + (col_of[:, None] - col_of[None, :] + side - 1)
    flat = table.reshape(table.shape[0], span * span).astype(jnp.float32)
    return jnp.take(flat, index, axis=1)

def attend(tokens, w_qkv, w_out, table):
    groups, count, width = tokens.shape
    heads = table.shape[0]
    size = width // heads
    normed = normalize(tokens)
    qkv = jnp.einsum('gtd,de->gte', normed.astype(jnp.float32), w_qkv.astype(jnp.float32)).astype(jnp.bfloat16)
    qkv = qkv.reshape(groups, count, 3, heads, size)
    query = qkv[:, :, 0].astype(jnp.float32)
    keys = qkv[:, :, 1].astype(jnp.float32)
    values = qkv[:, :, 2].astype(jnp.float32)
    scores = jnp.einsum('gshe,gthe->ghst', query, keys) * size ** (-0.5) + relative_bias(table)[None]
    weights = jax.nn.softmax(scores, axis=-1).astype(jnp.bfloat16)
    mixed = jnp.einsum('ghst,gthe->gshe', weights.astype(jnp.float32), values).astype(jnp.bfloat16)
    mixed = mixed.reshape(groups, count, width)
    added = jnp.einsum('gtd,de->gte', mixed.astype(jnp.float32), w_out.astype(jnp.float32))
    return (tokens.astype(jnp.float32) + added).astype(jnp.bfloat16)

def feed(tokens, w_in, w_out):
    normed = normalize(tokens)
    hidden = jax.nn.gelu(jnp.dot(normed, w_in, preferred_element_type=jnp.float32)).astype(jnp.bfloat16)
    added = jnp.dot(hidden, w_out.T, preferred_element_type=jnp.float32)
    return (tokens.astype(jnp.float32) + added).astype(jnp.bfloat16)

def reference(image, w_expand, dw_kernel, w_project, block_qkv, block_out, block_bias, mlp_in, mlp_out, grid_qkv, grid_out, grid_bias, mlp2_in, mlp2_out):
    height = ROWS_DEV * N_ROWS
    breadth = COLS_DEV * N_COLS
    cells = image.transpose(0, 2, 1)
    padded = jnp.pad(cells, ((1, 1), (1, 1), (0, 0)))

    def strip(index):
        rows_in = lax.dynamic_slice_in_dim(padded, index * ROWS_DEV, ROWS_DEV + 2, 0)
        expanded = jax.nn.gelu(jnp.dot(rows_in.reshape(-1, D), w_expand, preferred_element_type=jnp.float32))
        expanded = expanded.astype(jnp.bfloat16).reshape(ROWS_DEV + 2, breadth + 2, HID)
        conv = jnp.zeros((ROWS_DEV, breadth, HID), jnp.float32)
        for shift_r in range(3):
            for shift_c in range(3):
                conv = conv + expanded[shift_r:shift_r + ROWS_DEV, shift_c:shift_c + breadth].astype(jnp.float32) * dw_kernel[shift_r, shift_c].astype(jnp.float32)
        mobile = jax.nn.gelu(conv).astype(jnp.bfloat16)
        inner = rows_in[1:-1, 1:-1]
        added = jnp.dot(mobile.reshape(-1, HID), w_project.T, preferred_element_type=jnp.float32)
        stream = (inner.astype(jnp.float32) + added.reshape(ROWS_DEV, breadth, D)).astype(jnp.bfloat16)
        tiles = stream.reshape(ROWS_DEV // WIN, WIN, breadth // WIN, WIN, D).transpose(0, 2, 1, 3, 4)
        tiles = tiles.reshape(-1, WIN * WIN, D)
        tiles = attend(tiles, block_qkv, block_out, block_bias)
        stream = tiles.reshape(ROWS_DEV // WIN, breadth // WIN, WIN, WIN, D).transpose(0, 2, 1, 3, 4)
        stream = feed(stream.reshape(-1, D), mlp_in, mlp_out)
        return stream.reshape(ROWS_DEV, breadth, D)
    stream3 = lax.map(strip, jnp.arange(N_ROWS, dtype=jnp.int32)).reshape(height, breadth, D)
    stride_r = height // WIN
    stride_c = breadth // WIN
    grouped = stream3.reshape(WIN, stride_r, WIN, stride_c, D).transpose(1, 3, 0, 2, 4)

    def grid_row(block):
        tokens = block.reshape(stride_c, WIN * WIN, D)
        tokens = attend(tokens, grid_qkv, grid_out, grid_bias)
        tokens = feed(tokens.reshape(-1, D), mlp2_in, mlp2_out)
        return tokens.reshape(stride_c, WIN, WIN, D)
    done = lax.map(grid_row, grouped)
    return done.transpose(2, 0, 3, 1, 4).reshape(height, breadth, D).transpose(0, 2, 1)
```

```python
import functools
import math

import jax
import jax.numpy as jnp
from jax import lax
from jax.experimental import pallas as pl
from jax.experimental.pallas import tpu as pltpu
from jax.sharding import Mesh, PartitionSpec as P

WIN = 8
D = 192
HID = 768
HEADS = 6
SIZE = 32
COLS = 128
TOKENS = 64
QUAD = 256
ROWS_CHUNK = 8
N_CALLS = 2
LOG2E = 1.4426950408889634
F32 = jnp.float32
BF16 = jnp.bfloat16
NN = (((1,), (0,)), ((), ()))
NT = (((1,), (1,)), ((), ()))
TN = (((0,), (0,)), ((), ()))


def dot(a, b, dims=NN):
    return lax.dot_general(a, b, dims, preferred_element_type=F32)


def gelu(x):
    c0 = math.sqrt(2.0 / math.pi)
    inner = x * (c0 + (c0 * 0.044715) * (x * x))
    half = 0.5 * x
    return half + half * jnp.tanh(inner)


def norm(x):
    centre = x - jnp.mean(x, axis=-1, keepdims=True)
    spread = jnp.mean(centre * centre, axis=-1, keepdims=True)
    return (centre * lax.rsqrt(spread + 1e-05)).astype(BF16)


def mlp(s, w_in, w_out):
    hidden = gelu(dot(norm(s), w_in)).astype(BF16)
    return s + dot(hidden, w_out, NT)


def head_rows(q, heads):
    lane = lax.broadcasted_iota(jnp.int32, q.shape, 1) // SIZE
    zero = jnp.zeros_like(q)
    return jnp.concatenate([jnp.where(lane == h, q, zero) for h in range(heads)], axis=0)


def softmax_keys(scores):
    top = jnp.max(scores, axis=0, keepdims=True)
    weights = jnp.exp2(scores - top)
    total = jnp.sum(weights, axis=0, keepdims=True)
    return (weights * (1.0 / total)).astype(BF16)


def head_pick(out, heads):
    lane = lax.broadcasted_iota(jnp.int32, (TOKENS, out.shape[1]), 1) // SIZE
    got = out[:TOKENS]
    for h in range(1, heads):
        got = jnp.where(lane == h, out[h * TOKENS : (h + 1) * TOKENS], got)
    return got


def attend(s, wq, wk, wv, w_out, bias):
    n = norm(s)
    q = (dot(n, wq) * (SIZE**-0.5 * LOG2E)).astype(BF16)
    k = dot(n, wk).astype(BF16)
    v = dot(n, wv).astype(BF16)
    mixed = []
    for g in range(s.shape[0] // TOKENS):
        at = slice(g * TOKENS, (g + 1) * TOKENS)
        qg, kg, vg = q[at], k[at], v[at]
        parts = []
        for lo, hi, h0, h1 in ((0, 128, 0, 4), (128, 192, 4, 6)):
            count = h1 - h0
            scores = dot(kg[:, lo:hi], head_rows(qg[:, lo:hi], count), NT)
            scores = scores + bias[:, h0 * TOKENS : h1 * TOKENS]
            out = dot(softmax_keys(scores), vg[:, lo:hi], TN)
            parts.append(head_pick(out, count))
        mixed.append(jnp.concatenate(parts, axis=1).astype(BF16))
    return s + dot(jnp.concatenate(mixed, axis=0), w_out)


def split_qkv(w_ref, wq, wk, wv):
    wq[...] = w_ref[:, 0:D]
    wk[...] = w_ref[:, D : 2 * D]
    wv[...] = w_ref[:, 2 * D : 3 * D]


def first_kernel(
    first, last,
    image, before, after, top, bottom, left, right,
    w_expand, dw, w_project, w_qkv, w_out, bias, w_in, w_back,
    out, expanded, stream, side, wq, wk, wv,
):
    step = pl.program_id(0)
    steps = pl.num_programs(0)
    split_qkv(w_qkv, wq, wk, wv)

    def expand(row, x):
        tokens = x.T
        expanded[row] = gelu(dot(tokens, w_expand[...]))
        return tokens

    above = before[0]
    if first:
        above = jnp.where(step == 0, top[0], above)
    expand(0, above)
    expand(1, image[0])

    start = pl.multiple_of(step * ROWS_CHUNK, 8)
    for index, halo in enumerate((left, right)):
        cells = gelu(dot(halo[pl.ds(start, 16), :].astype(BF16), w_expand[...]))
        tap = 2 * index
        total = jnp.zeros((8, HID), F32)
        for i in range(3):
            total = total + cells[i : i + 8] * dw[3 * i + tap : 3 * i + tap + 1, :]
        for r in range(8):
            side[index, r] = jnp.broadcast_to(total[r : r + 1], (8, HID))

    def row(r, carry):
        below = image[jnp.minimum(r + 1, ROWS_CHUNK - 1)]
        edge = after[0]
        if last:
            edge = jnp.where(step == steps - 1, bottom[0], edge)
        expand(r + 2, jnp.where(r == ROWS_CHUNK - 1, edge, below))
        place = lax.broadcasted_iota(jnp.int32, (8, 128), 0)
        mobile = []
        for block in range(HID // 128):
            lanes = slice(block * 128, (block + 1) * 128)
            e = [expanded[r + i, :, lanes] for i in range(3)]
            taps = [
                sum(e[i] * dw[3 * i + k : 3 * i + k + 1, lanes] for i in range(3))
                for k in range(3)
            ]
            head = pltpu.roll(taps[0], 1, 0)
            tail = pltpu.roll(taps[2], COLS - 1, 0)
            head = jnp.concatenate(
                [jnp.where(place == 0, side[0, r, :, lanes], head[:8]), head[8:]], axis=0
            )
            tail = jnp.concatenate(
                [tail[:-8], jnp.where(place == 7, side[1, r, :, lanes], tail[-8:])], axis=0
            )
            mobile.append(gelu(head + taps[1] + tail).astype(BF16))
        mobile = jnp.concatenate(mobile, axis=1)
        tokens = image[r].T.astype(F32) + dot(mobile, w_project[...], NT)
        stream[:, r] = tokens.reshape(COLS // WIN, WIN, D)
        return carry

    lax.fori_loop(0, ROWS_CHUNK, row, 0)

    def windows(index, carry):
        at = pl.ds(index * 4, 4)
        s = stream[at].reshape(QUAD, D)
        s = attend(s, wq[...], wk[...], wv[...], w_out[...], bias)
        s = mlp(s, w_in[...], w_back[...])
        stream[at] = s.reshape(4, WIN, WIN, D)
        return carry

    lax.fori_loop(0, COLS // WIN // 4, windows, 0)

    for r in range(ROWS_CHUNK):
        rows = stream[:, r].reshape(2, 4, 16, D).astype(BF16)
        out[0, pl.ds(4 * r, 4), 0:16, :] = rows[0, :, :, 0:128]
        out[0, pl.ds(4 * r, 4), 16:32, :] = rows[1, :, :, 0:128]
        out[0, pl.ds(4 * r, 4), 32:48, :] = jnp.concatenate(
            [rows[0, :, :, 128:], rows[1, :, :, 128:]], axis=-1
        )


def grid_kernel(inp, w_qkv, w_out, bias, out, lo, hi, wq, wk, wv):
    split_qkv(w_qkv, wq, wk, wv)

    def load(src, carry):
        at = pl.multiple_of(src * 32, 32)
        lo[pl.ds(at, 32), :] = inp[0, src, 0:32, :].astype(F32)
        both = inp[0, src, 32:48, :].astype(F32)
        hi[pl.ds(at, 16), :] = both
        hi[pl.ds(at + 16, 16), :] = pltpu.roll(both, 64, 1)
        return carry

    lax.fori_loop(0, 32, load, 0)

    def groups(index, carry):
        first = index * 4
        picks = [pl.ds(first + g, TOKENS, stride=16) for g in range(4)]
        s = jnp.concatenate(
            [jnp.concatenate([lo[at, :], hi[at, :][:, :64]], axis=1) for at in picks], axis=0
        )
        s = attend(s, wq[...], wk[...], wv[...], w_out[...], bias)
        for g, at in enumerate(picks):
            rows = s[g * TOKENS : (g + 1) * TOKENS]
            lo[at, :] = rows[:, :128]
            hi[at, :] = jnp.concatenate([rows[:, 128:], rows[:, 128:]], axis=1)
        return carry

    lax.fori_loop(0, 4, groups, 0)

    def store(src, carry):
        at = pl.multiple_of(src * 32, 32)
        out[0, src, 0:32, :] = lo[pl.ds(at, 32), :].astype(BF16)
        lane = lax.broadcasted_iota(jnp.int32, (16, 128), 1)
        out[0, src, 32:48, :] = jnp.where(
            lane < 64, hi[pl.ds(at, 16), :], hi[pl.ds(at + 16, 16), :]
        ).astype(BF16)
        return carry

    lax.fori_loop(0, 32, store, 0)


def last_kernel(inp, w_in, w_back, out):
    def rows(index, carry):
        for half in range(2):
            r = 2 * index + half
            got = inp[0, pl.ds(4 * r, 4)].astype(F32)
            low = [got[:, 0:16], got[:, 16:32]]
            both = got[:, 32:48]
            high = [both[:, :, :64], both[:, :, 64:]]
            s = jnp.concatenate(
                [
                    jnp.concatenate([low[i].reshape(64, 128), high[i].reshape(64, 64)], axis=1)
                    for i in range(2)
                ],
                axis=0,
            )
            out[r] = mlp(s, w_in[...], w_back[...]).astype(BF16).T
        return carry

    lax.fori_loop(0, ROWS_CHUNK // 2, rows, 0)


def whole(shape):
    return pl.BlockSpec(shape, lambda k: (0,) * len(shape))


def vm(limit):
    return pltpu.CompilerParams(vmem_limit_bytes=limit << 20, dimension_semantics=("arbitrary",))


def call_first(call, chunks, image, top, bottom, left, right, weights):
    steps = chunks
    base = call * chunks
    total = image.shape[0]
    first, last = call == 0, (base + chunks) * ROWS_CHUNK == total
    rows = pl.BlockSpec((ROWS_CHUNK, D, COLS), lambda k: (base + k, 0, 0))
    before = pl.BlockSpec(
        (1, D, COLS), lambda k: (jnp.maximum((base + k) * ROWS_CHUNK - 1, 0), 0, 0)
    )
    after = pl.BlockSpec(
        (1, D, COLS), lambda k: (jnp.minimum((base + k + 1) * ROWS_CHUNK, total - 1), 0, 0)
    )
    left = left[base * ROWS_CHUNK : base * ROWS_CHUNK + chunks * ROWS_CHUNK + 8]
    right = right[base * ROWS_CHUNK : base * ROWS_CHUNK + chunks * ROWS_CHUNK + 8]
    small = [top, bottom, left, right] + weights
    tokens = chunks * ROWS_CHUNK * COLS
    return pl.pallas_call(
        functools.partial(first_kernel, first, last),
        grid=(steps,),
        in_specs=[rows, before, after] + [whole(a.shape) for a in small],
        out_specs=pl.BlockSpec((1, 32, 48, 128), lambda k: (k, 0, 0, 0)),
        out_shape=jax.ShapeDtypeStruct((chunks, 32, 48, 128), BF16),
        scratch_shapes=[
            pltpu.VMEM((ROWS_CHUNK + 2, COLS, HID), F32),
            pltpu.VMEM((COLS // WIN, WIN, WIN, D), F32),
            pltpu.VMEM((2, 8, 8, HID), F32),
            pltpu.VMEM((D, D), BF16),
            pltpu.VMEM((D, D), BF16),
            pltpu.VMEM((D, D), BF16),
        ],
        compiler_params=vm(48),
        cost_estimate=pl.CostEstimate(
            flops=tokens * 2000000, bytes_accessed=tokens * 800, transcendentals=tokens * 2700
        ),
        name="first",
    )(image, image, image, *small)


def call_grid(arrived, weights):
    chunks = arrived.shape[0]
    tokens = chunks * ROWS_CHUNK * COLS
    block = pl.BlockSpec((1, 32, 48, 128), lambda k: (k, 0, 0, 0))
    return pl.pallas_call(
        grid_kernel,
        grid=(chunks,),
        in_specs=[block] + [whole(a.shape) for a in weights],
        out_specs=block,
        out_shape=jax.ShapeDtypeStruct(arrived.shape, BF16),
        scratch_shapes=[
            pltpu.VMEM((1024, 128), F32),
            pltpu.VMEM((1024, 128), F32),
            pltpu.VMEM((D, D), BF16),
            pltpu.VMEM((D, D), BF16),
            pltpu.VMEM((D, D), BF16),
        ],
        compiler_params=vm(32),
        cost_estimate=pl.CostEstimate(
            flops=tokens * 500000, bytes_accessed=tokens * 800, transcendentals=tokens * 400
        ),
        name="grid",
    )(arrived, *weights)


def call_last(returned, w_in, w_back):
    chunks = returned.shape[0]
    tokens = chunks * ROWS_CHUNK * COLS
    return pl.pallas_call(
        last_kernel,
        grid=(chunks,),
        in_specs=[
            pl.BlockSpec((1, 32, 48, 128), lambda k: (k, 0, 0, 0)),
            whole(w_in.shape),
            whole(w_back.shape),
        ],
        out_specs=pl.BlockSpec((ROWS_CHUNK, D, COLS), lambda k: (k, 0, 0)),
        out_shape=jax.ShapeDtypeStruct((chunks * ROWS_CHUNK, D, COLS), BF16),
        compiler_params=vm(32),
        cost_estimate=pl.CostEstimate(
            flops=tokens * 600000, bytes_accessed=tokens * 800, transcendentals=tokens * 800
        ),
        name="last",
    )(returned, w_in, w_back)


def bias_rows(table):
    span = 2 * WIN - 1
    cols = jnp.stack([table[:, :, 7 - v : 15 - v] for v in range(WIN)], axis=0)
    both = jnp.stack([cols[:, :, 7 - u : 15 - u, :] for u in range(WIN)], axis=0)
    return both.reshape(TOKENS, HEADS * TOKENS) * LOG2E


def shift(x, axis, count, step):
    if step > 0:
        pairs = [(i, i + 1) for i in range(count - 1)]
    else:
        pairs = [(i + 1, i) for i in range(count - 1)]
    return lax.ppermute(x, axis, pairs)


ROW_AXES = ("y", "zh", "zl", "xl")
COL_AXES = ("xh", "core")
GROUP = ("y", "zh", "xh", "core")


def body(
    image, w_expand, dw_kernel, w_project, block_qkv, block_out, block_bias, mlp_in, mlp_out,
    grid_qkv, grid_out, grid_bias, mlp2_in, mlp2_out,
):
    rows = image.shape[0]
    top = shift(image[rows - 1 :], ROW_AXES, 32, 1)
    bottom = shift(image[:1], ROW_AXES, 32, -1)
    ends = [
        jnp.concatenate([top[:, :, c], image[:, :, c], bottom[:, :, c]], axis=0)
        for c in (0, COLS - 1)
    ]
    left = shift(ends[1], COL_AXES, 4, 1)
    right = shift(ends[0], COL_AXES, 4, -1)
    left = jnp.pad(left.astype(F32), ((0, 6), (0, 0)))
    right = jnp.pad(right.astype(F32), ((0, 6), (0, 0)))
    bias1 = bias_rows(block_bias)
    bias2 = bias_rows(grid_bias)
    weights = [
        w_expand, dw_kernel.reshape(9, HID).astype(F32), w_project, block_qkv, block_out, bias1,
        mlp_in, mlp_out,
    ]
    chunks = rows // ROWS_CHUNK // N_CALLS
    outs = []
    for call in range(N_CALLS):
        sent = call_first(call, chunks, image, top, bottom, left, right, weights)
        arrived = lax.all_to_all(sent, GROUP, 1, 1, tiled=True)
        mixed = call_grid(arrived, [grid_qkv, grid_out, bias2])
        back = lax.all_to_all(mixed, GROUP, 1, 1, tiled=True)
        outs.append(call_last(back, mlp2_in, mlp2_out))
    return jnp.concatenate(outs, axis=0)


def solution(mesh):
    names = ("y", "zh", "zl", "xl", "xh", "core")
    fine = Mesh(mesh.devices.reshape(4, 2, 2, 2, 2, 2), names)
    spec = P(ROW_AXES, None, COL_AXES)
    return jax.shard_map(
        body, mesh=fine, in_specs=(spec,) + (P(),) * 13, out_specs=spec, check_vma=False
    )
```

```python
import functools
import math

import jax
import jax.numpy as jnp
from jax import lax
from jax.experimental import pallas as pl
from jax.experimental.pallas import tpu as pltpu
from jax.sharding import Mesh, PartitionSpec as P

WIN = 8
D = 192
HID = 768
HEADS = 6
SIZE = 32
COLS = 128
TOKENS = 64
CHUNK = 1024
ROWS_CHUNK = 8
TILES = 16
LAG = 3
CALLS = (2, 2)
LOG2E = 1.4426950408889634
F32 = jnp.float32
BF16 = jnp.bfloat16
NN = (((1,), (0,)), ((), ()))
NT = (((1,), (1,)), ((), ()))
TN = (((0,), (0,)), ((), ()))
C0 = math.sqrt(2.0 / math.pi)
C1 = 0.044715 * C0


def dot(a, b, dims=NN):
    return lax.dot_general(a, b, dims, preferred_element_type=F32)


def gelu(x):
    x = x.astype(BF16)
    inner = x * (BF16(C0) + BF16(C1) * (x * x))
    half = BF16(0.5) * x
    return half + half * jnp.tanh(inner)


def norm(s):
    centre = s - jnp.mean(s, axis=0, keepdims=True)
    spread = jnp.mean(centre * centre, axis=0, keepdims=True)
    return (centre * lax.rsqrt(spread + 1e-05)).astype(BF16)


def mlp(s, w_in_t, w_out):
    return s + dot(w_out, gelu(dot(w_in_t, norm(s))))


def softmax_keys(scores):
    top = jnp.max(scores, axis=0, keepdims=True)
    weights = jnp.exp2(scores - top)
    total = jnp.sum(weights, axis=0, keepdims=True)
    return (weights * (1.0 / total)).astype(BF16)


def attend(s, wq_t, wk, wv_t, w_out_t, bias):
    n = norm(s)
    q = dot(wq_t, n) * (SIZE**-0.5 * LOG2E)
    v = dot(wv_t, n).astype(BF16)
    k = dot(n, wk, TN).astype(BF16)
    left = lax.broadcasted_iota(jnp.int32, (1, 128), 1) < TOKENS
    keep = (lax.broadcasted_iota(jnp.int32, (TOKENS, 1), 0) < SIZE) == left
    zero = jnp.zeros((TOKENS, 128), BF16)
    tiles = s.shape[1] // 128
    ready = {}
    mixed = []

    def score(t):
        here = q[:, 128 * t : 128 * t + 128]
        swapped = pltpu.roll(here, TOKENS, 1).astype(BF16)
        here = here.astype(BF16)
        got = []
        for g in range(2):
            both = jnp.where(left, here, swapped) if g == 0 else jnp.where(left, swapped, here)
            keys = k[(2 * t + g) * TOKENS : (2 * t + g + 1) * TOKENS]
            b = [jnp.where(keep, both[64 * p : 64 * p + 64], zero) for p in range(3)]
            four = jnp.concatenate(
                [jnp.concatenate([b[0], zero], axis=1), jnp.concatenate([zero, b[1]], axis=1)],
                axis=0,
            )
            first = softmax_keys(dot(keys[:, :128], four) + bias[:, :256])
            last = softmax_keys(dot(keys[:, 128:], b[2]) + bias[:, 256:])
            got.append((first[:, :128], first[:, 128:], last))
        ready[t] = got

    def mix(t):
        got = ready.pop(t)
        values = v[:, 128 * t : 128 * t + 128]
        rows = []
        for p in range(3):
            pair = jnp.concatenate(
                [
                    jnp.concatenate([got[0][p], zero], axis=1),
                    jnp.concatenate([zero, got[1][p]], axis=1),
                ],
                axis=0,
            )
            out = dot(values[64 * p : 64 * p + 64], pair)
            a, b = out[:, :128], out[:, 128:]
            rows.append(jnp.where(left, a[:SIZE], pltpu.roll(b[:SIZE], TOKENS, 1)))
            rows.append(jnp.where(left, pltpu.roll(a[SIZE:], TOKENS, 1), b[SIZE:]))
        mixed.append(jnp.concatenate(rows, axis=0).astype(BF16))

    for t in range(tiles + LAG):
        if t < tiles:
            score(t)
        if t >= LAG:
            mix(t - LAG)
    return s + dot(w_out_t, jnp.concatenate(mixed, axis=1))


def prepare(w_qkv, w_out, table, wq_t, wk, wv_t, w_out_t, bias):
    wq_t[...] = w_qkv[:, 0:D].T
    wk[...] = w_qkv[:, D : 2 * D]
    wv_t[...] = w_qkv[:, 2 * D : 3 * D].T
    w_out_t[...] = w_out[...].T
    left = lax.broadcasted_iota(jnp.int32, (WIN, 128), 1) < TOKENS
    for u in range(WIN):
        for p in range(3):
            start = (7 - u) * WIN
            even = pltpu.roll(table[2 * p], (128 - start) % 128, 1)
            odd = pltpu.roll(table[2 * p + 1], (64 - start) % 128, 1)
            bias[u * WIN : (u + 1) * WIN, 128 * p : 128 * p + 128] = (
                jnp.where(left, even, odd) * LOG2E
            )


def gather_groups(lo, hi):
    parts = []
    for g in range(TILES):
        at = pl.ds(g, TOKENS, stride=TILES)
        parts.append(jnp.concatenate([lo[at, :], hi[at, :][:, :64]], axis=1))
    return jnp.concatenate(parts, axis=0).T


def first_kernel(
    first, last,
    image, before, after, top, bottom, left, right,
    w_expand, dw, w_project, w_qkv, w_out, table, w_in, w_back,
    out, expanded, mobile, tokens, lo, hi, place, wq_t, wk, wv_t, w_out_t, w_in_t, bias,
):
    step = pl.program_id(0)
    steps = pl.num_programs(0)
    start = pl.multiple_of(step * ROWS_CHUNK, 8)
    line = lax.broadcasted_iota(jnp.int32, (16, HID), 0)

    def laid(x):
        return dot(place[...], x, NT).astype(BF16)

    def expand(x, sides, rows):
        cells = gelu(dot(x, w_expand[...])).astype(F32)
        for i, r in enumerate(rows):
            e = cells[COLS * i : COLS * (i + 1)]
            expanded[r, 16:144, :] = e
            prev = pltpu.roll(e[112:128], 1, 0)
            expanded[r, 0:16, :] = jnp.where(line == 0, sides[0][r : r + 1], prev)
            follow = pltpu.roll(e[0:16], 15, 0)
            expanded[r, 144:160, :] = jnp.where(line == 15, sides[1][r : r + 1], follow)

    sides = [
        gelu(dot(halo[pl.ds(start, 16), :].astype(BF16), w_expand[...])).astype(F32)
        for halo in (left, right)
    ]

    @pl.when(step == 0)
    def _():
        prepare(w_qkv, w_out, table, wq_t, wk, wv_t, w_out_t, bias)
        w_in_t[...] = w_in[...].T
        row = lax.broadcasted_iota(jnp.int32, (COLS, COLS), 0)
        col = lax.broadcasted_iota(jnp.int32, (COLS, COLS), 1)
        place[...] = jnp.where(col == (row % 16) * 8 + row // 16, 1.0, 0.0).astype(BF16)
        above = top[0] if first else before[0]
        pair = jnp.concatenate([laid(above), laid(image[0])], axis=0)
        tokens[0:COLS, :] = pair[COLS:]
        expand(pair, sides, (0, 1))

    @pl.when(step > 0)
    def _():
        tokens[0:COLS, :] = tokens[8 * COLS : 9 * COLS, :]
        expanded[0:2] = expanded[8:10]

    below = after[0]
    if last:
        below = jnp.where(step == steps - 1, bottom[0], below)
    for r in range(1, ROWS_CHUNK):
        tokens[COLS * r : COLS * (r + 1), :] = laid(image[r])
    tokens[COLS * 8 : COLS * 9, :] = laid(below)
    for half in range(2):
        x = tokens[COLS * (1 + 4 * half) : COLS * (5 + 4 * half), :]
        expand(x, sides, range(2 + 4 * half, 6 + 4 * half))

    for r in range(ROWS_CHUNK):
        for block in range(HID // 128):
            lanes = slice(block * 128, (block + 1) * 128)
            conv = None
            for i in range(3):
                for k in range(3):
                    term = expanded[r + i, 16 * k : 16 * k + COLS, lanes] * dw[
                        3 * i + k : 3 * i + k + 1, lanes
                    ]
                    conv = term if conv is None else conv + term
            mobile[COLS * r : COLS * (r + 1), lanes] = gelu(conv)

    s = tokens[0:CHUNK, :].astype(F32) + dot(mobile[...], w_project[...], NT)
    lo[...] = s[:, :128]
    hi[:, :64] = s[:, 128:]
    s = gather_groups(lo, hi)
    s = attend(s, wq_t[...], wk[...], wv_t[...], w_out_t[...], bias)
    s = mlp(s, w_in_t[...], w_back[...]).T.reshape(TILES, WIN, WIN, D)
    for r in range(ROWS_CHUNK):
        rows = s[:, r].reshape(2, 4, 16, D)
        at = slice(4 * r, 4 * r + 4)
        out[at, 0, 0:16, :] = rows[0, :, :, 0:128].astype(BF16)
        out[at, 0, 16:32, :] = rows[1, :, :, 0:128].astype(BF16)
        out[at, 0, 32:48, :] = jnp.concatenate(
            [rows[0, :, :, 128:], rows[1, :, :, 128:]], axis=-1
        ).astype(BF16)


def grid_kernel(
    inp, w_qkv, w_out, table, out, lo, hi, wq_t, wk, wv_t, w_out_t, bias
):
    @pl.when(pl.program_id(0) == 0)
    def _():
        prepare(w_qkv, w_out, table, wq_t, wk, wv_t, w_out_t, bias)

    for src in range(32):
        lo[32 * src : 32 * src + 32, :] = inp[src, 0, 0:32, :].astype(F32)
        both = inp[src, 0, 32:48, :].astype(F32)
        hi[32 * src : 32 * src + 16, :] = both
        hi[32 * src + 16 : 32 * src + 32, :] = pltpu.roll(both, 64, 1)
    s = gather_groups(lo, hi)
    s = attend(s, wq_t[...], wk[...], wv_t[...], w_out_t[...], bias).T
    for g in range(TILES):
        at = pl.ds(g, TOKENS, stride=TILES)
        rows = s[g * TOKENS : (g + 1) * TOKENS]
        lo[at, :] = rows[:, :128]
        hi[at, :] = jnp.concatenate([rows[:, 128:], rows[:, 128:]], axis=1)
    left = lax.broadcasted_iota(jnp.int32, (16, 128), 1) < 64
    for src in range(32):
        out[src, 0, 0:32, :] = lo[32 * src : 32 * src + 32, :].astype(BF16)
        out[src, 0, 32:48, :] = jnp.where(
            left, hi[32 * src : 32 * src + 16, :], hi[32 * src + 16 : 32 * src + 32, :]
        ).astype(BF16)


def last_kernel(inp, w_in, w_back, *rest):
    out, w_in_t = rest[-2:]

    @pl.when(pl.program_id(0) == 0)
    def _():
        w_in_t[...] = w_in[...].T

    rows = []
    for r in range(ROWS_CHUNK):
        got = inp[4 * r : 4 * r + 4, 0].astype(F32)
        both = got[:, 32:48].reshape(64, 128)
        for i in range(2):
            low = got[:, 16 * i : 16 * i + 16].reshape(64, 128)
            rows.append(jnp.concatenate([low, both[:, 64 * i : 64 * i + 64]], axis=1))
    s = jnp.concatenate(rows, axis=0).T
    s = mlp(s, w_in_t[...], w_back[...]).astype(BF16)
    for r in range(ROWS_CHUNK):
        out[r] = s[:, COLS * r : COLS * (r + 1)]


def whole(shape):
    return pl.BlockSpec(shape, lambda k: (0,) * len(shape))


def vm(limit):
    return pltpu.CompilerParams(vmem_limit_bytes=limit << 20, dimension_semantics=("arbitrary",))


BLOCK = pl.BlockSpec((32, 1, 48, 128), lambda k: (0, k, 0, 0))
ATTEND_SCRATCH = [
    pltpu.VMEM((D, D), BF16),
    pltpu.VMEM((D, D), BF16),
    pltpu.VMEM((D, D), BF16),
    pltpu.VMEM((D, D), BF16),
]


def call_first(base, chunks, image, top, bottom, left, right, weights):
    total = image.shape[0]
    first, last = base == 0, (base + chunks) * ROWS_CHUNK == total
    rows = pl.BlockSpec((ROWS_CHUNK, D, COLS), lambda k: (base + k, 0, 0))
    before = pl.BlockSpec((1, D, COLS), lambda k: (max(base * ROWS_CHUNK - 1, 0), 0, 0))
    after = pl.BlockSpec(
        (1, D, COLS), lambda k: (jnp.minimum((base + k + 1) * ROWS_CHUNK, total - 1), 0, 0)
    )
    at = slice(base * ROWS_CHUNK, (base + chunks) * ROWS_CHUNK + 8)
    small = [top, bottom, left[at], right[at]] + weights
    tokens = chunks * CHUNK
    return pl.pallas_call(
        functools.partial(first_kernel, first, last),
        grid=(chunks,),
        in_specs=[rows, before, after] + [whole(a.shape) for a in small],
        out_specs=BLOCK,
        out_shape=jax.ShapeDtypeStruct((32, chunks, 48, 128), BF16),
        scratch_shapes=[
            pltpu.VMEM((ROWS_CHUNK + 2, 160, HID), F32),
            pltpu.VMEM((CHUNK, HID), BF16),
            pltpu.VMEM((9 * COLS, D), BF16),
            pltpu.VMEM((CHUNK, 128), F32),
            pltpu.VMEM((CHUNK, 128), F32),
            pltpu.VMEM((COLS, COLS), BF16),
        ]
        + ATTEND_SCRATCH
        + [pltpu.VMEM((HID, D), BF16), pltpu.VMEM((TOKENS, HEADS * TOKENS), F32)],
        compiler_params=vm(48),
        cost_estimate=pl.CostEstimate(
            flops=tokens * 2000000, bytes_accessed=tokens * 800, transcendentals=tokens * 2700
        ),
        name="first",
    )(image, image, image, *small)


def call_grid(arrived, weights):
    chunks = arrived.shape[1]
    tokens = chunks * CHUNK
    return pl.pallas_call(
        grid_kernel,
        grid=(chunks,),
        in_specs=[BLOCK] + [whole(a.shape) for a in weights],
        out_specs=BLOCK,
        out_shape=jax.ShapeDtypeStruct(arrived.shape, BF16),
        scratch_shapes=[pltpu.VMEM((CHUNK, 128), F32), pltpu.VMEM((CHUNK, 128), F32)]
        + ATTEND_SCRATCH
        + [pltpu.VMEM((TOKENS, HEADS * TOKENS), F32)],
        compiler_params=vm(32),
        cost_estimate=pl.CostEstimate(
            flops=tokens * 1000000, bytes_accessed=tokens * 800, transcendentals=tokens * 400
        ),
        name="grid",
    )(arrived, *weights)


def call_last(base, rows, returned, w_in, w_back, earlier):
    chunks = returned.shape[1]
    tokens = chunks * CHUNK
    operands = [returned, w_in, w_back]
    specs = [BLOCK, whole(w_in.shape), whole(w_back.shape)]
    aliases = {}
    if earlier is not None:
        operands.append(earlier)
        specs.append(pl.BlockSpec(memory_space=pl.ANY))
        aliases = {3: 0}
    return pl.pallas_call(
        last_kernel,
        grid=(chunks,),
        in_specs=specs,
        out_specs=pl.BlockSpec((ROWS_CHUNK, D, COLS), lambda k: (base + k, 0, 0)),
        out_shape=jax.ShapeDtypeStruct((rows, D, COLS), BF16),
        scratch_shapes=[pltpu.VMEM((HID, D), BF16)],
        input_output_aliases=aliases,
        compiler_params=vm(32),
        cost_estimate=pl.CostEstimate(
            flops=tokens * 1000000, bytes_accessed=tokens * 800, transcendentals=tokens * 800
        ),
        name="last",
    )(*operands)


def bias_tables(tables):
    cols = jnp.stack([tables[:, :, 7 - v : 15 - v] for v in range(WIN)], axis=1)
    return jnp.pad(cols.reshape(2 * HEADS, WIN, 15 * WIN), ((0, 0), (0, 0), (0, 8)))


def shift(x, axis, count, step):
    if step > 0:
        pairs = [(i, i + 1) for i in range(count - 1)]
    else:
        pairs = [(i + 1, i) for i in range(count - 1)]
    return lax.ppermute(x, axis, pairs)


ROW_AXES = ("y", "zh", "zl", "xl")
COL_AXES = ("xh", "core")
GROUP = ("y", "zh", "xh", "core")


def body(
    image, w_expand, dw_kernel, w_project, block_qkv, block_out, block_bias, mlp_in, mlp_out,
    grid_qkv, grid_out, grid_bias, mlp2_in, mlp2_out,
):
    rows = image.shape[0]
    top = shift(image[rows - 1 :], ROW_AXES, 32, 1)
    bottom = shift(image[:1], ROW_AXES, 32, -1)
    ends = [
        jnp.concatenate([top[:, :, c], image[:, :, c], bottom[:, :, c]], axis=0)
        for c in (0, COLS - 1)
    ]
    left = shift(ends[1], COL_AXES, 4, 1)
    right = shift(ends[0], COL_AXES, 4, -1)
    left = jnp.pad(left.astype(F32), ((0, 6), (0, 0)))
    right = jnp.pad(right.astype(F32), ((0, 6), (0, 0)))
    tables = bias_tables(jnp.concatenate([block_bias, grid_bias], axis=0))
    weights = [
        w_expand, dw_kernel.reshape(9, HID).astype(F32), w_project, block_qkv, block_out,
        tables[:HEADS], mlp_in, mlp_out,
    ]
    base = 0
    result = None
    for chunks in CALLS:
        sent = call_first(base, chunks, image, top, bottom, left, right, weights)
        arrived = lax.all_to_all(sent, GROUP, 0, 0, tiled=True)
        mixed = call_grid(arrived, [grid_qkv, grid_out, tables[HEADS:]])
        back = lax.all_to_all(mixed, GROUP, 0, 0, tiled=True)
        result = call_last(base, rows, back, mlp2_in, mlp2_out, result)
        base += chunks
    return result


def solution(mesh):
    names = ("y", "zh", "zl", "xl", "xh", "core")
    fine = Mesh(mesh.devices.reshape(4, 2, 2, 2, 2, 2), names)
    spec = P(ROW_AXES, None, COL_AXES)
    return jax.shard_map(
        body, mesh=fine, in_specs=(spec,) + (P(),) * 13, out_specs=spec, check_vma=False
    )
```

```python
import functools
import math

import jax
import jax.numpy as jnp
from jax import lax
from jax.experimental import pallas as pl
from jax.experimental.pallas import tpu as pltpu
from jax.sharding import Mesh, PartitionSpec as P

WIN = 8
D = 192
HID = 768
HEADS = 6
SIZE = 32
COLS = 128
TOKENS = 64
CHUNK = 1024
ROWS_CHUNK = 8
TILES = 16
LAG = 3
LOG2E = 1.4426950408889634
F32 = jnp.float32
BF16 = jnp.bfloat16
NN = (((1,), (0,)), ((), ()))
NT = (((1,), (1,)), ((), ()))
TN = (((0,), (0,)), ((), ()))
C0 = math.sqrt(2.0 / math.pi)
C1 = 0.044715 * C0


def dot(a, b, dims=NN):
    return lax.dot_general(a, b, dims, preferred_element_type=F32)


def gelu(x):
    x = x.astype(BF16)
    inner = x * (BF16(C0) + BF16(C1) * (x * x))
    half = BF16(0.5) * x
    return half + half * jnp.tanh(inner)


def norm(s):
    centre = s - jnp.mean(s, axis=0, keepdims=True)
    spread = jnp.mean(centre * centre, axis=0, keepdims=True)
    return (centre * lax.rsqrt(spread + 1e-05)).astype(BF16)


def mlp(s, w_in_t, w_out):
    return s + dot(w_out, gelu(dot(w_in_t, norm(s))))


def softmax_keys(scores):
    top = jnp.max(scores, axis=0, keepdims=True)
    weights = jnp.exp2(scores - top)
    total = jnp.sum(weights, axis=0, keepdims=True)
    return (weights * (1.0 / total)).astype(BF16)


def attend(s, wq_t, wk, wv_t, w_out_t, bias):
    n = norm(s)
    q = dot(wq_t, n) * (SIZE**-0.5 * LOG2E)
    v = dot(wv_t, n).astype(BF16)
    k = dot(n, wk, TN).astype(BF16)
    left = lax.broadcasted_iota(jnp.int32, (1, 128), 1) < TOKENS
    keep = (lax.broadcasted_iota(jnp.int32, (TOKENS, 1), 0) < SIZE) == left
    zero = jnp.zeros((TOKENS, 128), BF16)
    tiles = s.shape[1] // 128
    ready = {}
    mixed = []

    def score(t):
        here = q[:, 128 * t : 128 * t + 128]
        swapped = pltpu.roll(here, TOKENS, 1).astype(BF16)
        here = here.astype(BF16)
        got = []
        for g in range(2):
            both = jnp.where(left, here, swapped) if g == 0 else jnp.where(left, swapped, here)
            keys = k[(2 * t + g) * TOKENS : (2 * t + g + 1) * TOKENS]
            b = [jnp.where(keep, both[64 * p : 64 * p + 64], zero) for p in range(3)]
            four = jnp.concatenate(
                [jnp.concatenate([b[0], zero], axis=1), jnp.concatenate([zero, b[1]], axis=1)],
                axis=0,
            )
            first = softmax_keys(dot(keys[:, :128], four) + bias[:, :256])
            last = softmax_keys(dot(keys[:, 128:], b[2]) + bias[:, 256:])
            got.append((first[:, :128], first[:, 128:], last))
        ready[t] = got

    def mix(t):
        got = ready.pop(t)
        values = v[:, 128 * t : 128 * t + 128]
        rows = []
        for p in range(3):
            pair = jnp.concatenate(
                [
                    jnp.concatenate([got[0][p], zero], axis=1),
                    jnp.concatenate([zero, got[1][p]], axis=1),
                ],
                axis=0,
            )
            out = dot(values[64 * p : 64 * p + 64], pair)
            a, b = out[:, :128], out[:, 128:]
            rows.append(jnp.where(left, a[:SIZE], pltpu.roll(b[:SIZE], TOKENS, 1)))
            rows.append(jnp.where(left, pltpu.roll(a[SIZE:], TOKENS, 1), b[SIZE:]))
        mixed.append(jnp.concatenate(rows, axis=0).astype(BF16))

    for t in range(tiles + LAG):
        if t < tiles:
            score(t)
        if t >= LAG:
            mix(t - LAG)
    return s + dot(w_out_t, jnp.concatenate(mixed, axis=1))


def bias_rows(table, padded, bias):
    lane = lax.broadcasted_iota(jnp.int32, (16, 128), 1)
    line = lax.broadcasted_iota(jnp.int32, (16, 128), 0)
    spread = jnp.where(lane // WIN == line, 1.0, 0.0)
    left = lax.broadcasted_iota(jnp.int32, (WIN, 128), 1) < TOKENS
    padded[...] = jnp.zeros_like(padded)
    heads = []
    for h in range(HEADS):
        padded[h, 0:15, 0:15] = table[h]
        cells = lax.dot_general(
            padded[h][:, :16], spread, TN, precision=lax.Precision.HIGHEST,
            preferred_element_type=F32,
        )
        rows = [
            jnp.sum(jnp.where(line == 7 - v + lane % WIN, cells, 0.0), axis=0, keepdims=True)
            for v in range(WIN)
        ]
        heads.append(jnp.concatenate(rows, axis=0))
    for u in range(WIN):
        for p in range(3):
            start = (7 - u) * WIN
            even = pltpu.roll(heads[2 * p], (128 - start) % 128, 1)
            odd = pltpu.roll(heads[2 * p + 1], (64 - start) % 128, 1)
            bias[u * WIN : (u + 1) * WIN, 128 * p : 128 * p + 128] = (
                jnp.where(left, even, odd) * LOG2E
            )


def prepare(w_qkv, w_out, table, wq_t, wk, wv_t, w_out_t, bias, padded):
    wq_t[...] = w_qkv[:, 0:D].T
    wk[...] = w_qkv[:, D : 2 * D]
    wv_t[...] = w_qkv[:, 2 * D : 3 * D].T
    w_out_t[...] = w_out[...].T
    bias_rows(table, padded, bias)


def gather_groups(lo, hi):
    parts = []
    for g in range(TILES):
        at = pl.ds(g, TOKENS, stride=TILES)
        parts.append(jnp.concatenate([lo[at, :], hi[at, :][:, :64]], axis=1))
    return jnp.concatenate(parts, axis=0).T


def first_kernel(
    edge, image, before, after, top, bottom, left, right,
    w_expand, taps, w_project, w_qkv, w_out, table, w_in, w_back,
    out, expanded, mobile, tokens, lo, hi, place, wq_t, wk, wv_t, w_out_t, w_in_t, bias, padded,
    dw, side,
):
    step = pl.program_id(0)
    line = lax.broadcasted_iota(jnp.int32, (16, HID), 0)

    def laid(x):
        return dot(place[...], x, NT).astype(BF16)

    def expand(x, sides, rows):
        cells = gelu(dot(x, w_expand[...])).astype(F32)
        for i, r in enumerate(rows):
            e = cells[COLS * i : COLS * (i + 1)]
            expanded[r, 16:144, :] = e
            prev = pltpu.roll(e[112:128], 1, 0)
            expanded[r, 0:16, :] = jnp.where(line == 0, sides[0][r : r + 1], prev)
            follow = pltpu.roll(e[0:16], 15, 0)
            expanded[r, 144:160, :] = jnp.where(line == 15, sides[1][r : r + 1], follow)

    @pl.when(step == 0)
    def _():
        for i in range(3):
            dw[3 * i : 3 * i + 3, :] = taps[i].astype(F32)
        for i, halo in enumerate((left, right)):
            side[i, 8:40, :] = gelu(dot(halo[...], w_expand[...])).astype(F32)
            if edge:
                for j, message in enumerate((top, bottom)):
                    pair = message[D + 32 * i : D + 32 * i + 32, :]
                    corner = jnp.concatenate([pair[0:16], pair[16:32, 0:64]], axis=1)
                    ends = gelu(dot(corner, w_expand[...])).astype(F32)
                    side[i, 40 * j : 40 * j + 8, :] = jnp.broadcast_to(ends[0:1], (8, HID))
        prepare(w_qkv, w_out, table, wq_t, wk, wv_t, w_out_t, bias, padded)
        w_in_t[...] = w_in[...].T
        row = lax.broadcasted_iota(jnp.int32, (COLS, COLS), 0)
        col = lax.broadcasted_iota(jnp.int32, (COLS, COLS), 1)
        place[...] = jnp.where(col == (row % 16) * 8 + row // 16, 1.0, 0.0).astype(BF16)

    order = (step + 1) if not edge else jnp.where(step == 0, 3, 0)
    start = pl.multiple_of(order * ROWS_CHUNK, 8)
    sides = [side[i, pl.ds(start, 24), :][7:23] for i in range(2)]

    def begin():
        above = before[0]
        if edge:
            above = jnp.where(step == 0, above, top[0:D, :])
        pair = jnp.concatenate([laid(above), laid(image[0])], axis=0)
        tokens[0:COLS, :] = pair[COLS:]
        expand(pair, sides, (0, 1))

    below = after[0]
    if edge:
        below = jnp.where(step == 0, bottom[0:D, :], below)
        begin()
    else:
        pl.when(step == 0)(begin)

        @pl.when(step > 0)
        def _():
            tokens[0:COLS, :] = tokens[8 * COLS : 9 * COLS, :]
            expanded[0:2] = expanded[8:10]

    for r in range(1, ROWS_CHUNK):
        tokens[COLS * r : COLS * (r + 1), :] = laid(image[r])
    tokens[COLS * 8 : COLS * 9, :] = laid(below)
    for half in range(2):
        x = tokens[COLS * (1 + 4 * half) : COLS * (5 + 4 * half), :]
        expand(x, sides, range(2 + 4 * half, 6 + 4 * half))

    for r in range(ROWS_CHUNK):
        for block in range(HID // 128):
            lanes = slice(block * 128, (block + 1) * 128)
            conv = None
            for i in range(3):
                for k in range(3):
                    term = expanded[r + i, 16 * k : 16 * k + COLS, lanes] * dw[
                        3 * i + k : 3 * i + k + 1, lanes
                    ]
                    conv = term if conv is None else conv + term
            mobile[COLS * r : COLS * (r + 1), lanes] = gelu(conv)

    s = tokens[0:CHUNK, :].astype(F32) + dot(mobile[...], w_project[...], NT)
    lo[...] = s[:, :128]
    hi[:, :64] = s[:, 128:]
    s = gather_groups(lo, hi)
    s = attend(s, wq_t[...], wk[...], wv_t[...], w_out_t[...], bias)
    s = mlp(s, w_in_t[...], w_back[...]).T.reshape(TILES, WIN, WIN, D)
    for r in range(ROWS_CHUNK):
        rows = s[:, r].reshape(2, 4, 16, D)
        at = slice(4 * r, 4 * r + 4)
        out[at, 0, 0:16, :] = rows[0, :, :, 0:128].astype(BF16)
        out[at, 0, 16:32, :] = rows[1, :, :, 0:128].astype(BF16)
        out[at, 0, 32:48, :] = jnp.concatenate(
            [rows[0, :, :, 128:], rows[1, :, :, 128:]], axis=-1
        ).astype(BF16)


def grid_kernel(
    one, two, w_qkv, w_out, table, out, lo, hi, wq_t, wk, wv_t, w_out_t, bias, padded
):
    step = pl.program_id(0)

    @pl.when(step == 0)
    def _():
        prepare(w_qkv, w_out, table, wq_t, wk, wv_t, w_out_t, bias, padded)

    def unpack(inp):
        for src in range(32):
            lo[32 * src : 32 * src + 32, :] = inp[src, 0, 0:32, :].astype(F32)
            both = inp[src, 0, 32:48, :].astype(F32)
            hi[32 * src : 32 * src + 16, :] = both
            hi[32 * src + 16 : 32 * src + 32, :] = pltpu.roll(both, 64, 1)

    pl.when(step < 2)(lambda: unpack(one))
    pl.when(step >= 2)(lambda: unpack(two))
    s = gather_groups(lo, hi)
    s = attend(s, wq_t[...], wk[...], wv_t[...], w_out_t[...], bias).T
    for g in range(TILES):
        at = pl.ds(g, TOKENS, stride=TILES)
        rows = s[g * TOKENS : (g + 1) * TOKENS]
        lo[at, :] = rows[:, :128]
        hi[at, :] = jnp.concatenate([rows[:, 128:], rows[:, 128:]], axis=1)
    left = lax.broadcasted_iota(jnp.int32, (16, 128), 1) < 64
    for src in range(32):
        out[src, 0, 0:32, :] = lo[32 * src : 32 * src + 32, :].astype(BF16)
        out[src, 0, 32:48, :] = jnp.where(
            left, hi[32 * src : 32 * src + 16, :], hi[32 * src + 16 : 32 * src + 32, :]
        ).astype(BF16)


def last_kernel(inp, w_in, w_back, out, w_in_t):
    @pl.when(pl.program_id(0) == 0)
    def _():
        w_in_t[...] = w_in[...].T

    rows = []
    for r in range(ROWS_CHUNK):
        got = inp[4 * r : 4 * r + 4, 0].astype(F32)
        both = got[:, 32:48].reshape(64, 128)
        for i in range(2):
            low = got[:, 16 * i : 16 * i + 16].reshape(64, 128)
            rows.append(jnp.concatenate([low, both[:, 64 * i : 64 * i + 64]], axis=1))
    s = jnp.concatenate(rows, axis=0).T
    s = mlp(s, w_in_t[...], w_back[...]).astype(BF16)
    for r in range(ROWS_CHUNK):
        out[r] = s[:, COLS * r : COLS * (r + 1)]


def pack_kernel(lowest, highest, left, right, down, up):
    for r, cells, out in ((left.shape[0] - 1, lowest, down), (0, highest, up)):
        out[0:D, :] = cells[0]
        for i, halo in enumerate((left, right)):
            cell = halo[r : r + 1, :].astype(F32)
            high = jnp.concatenate([cell[:, 128:], cell[:, 128:]], axis=1)
            at = D + 32 * i
            out[at : at + 16, :] = jnp.broadcast_to(cell[:, :128], (16, 128)).astype(BF16)
            out[at + 16 : at + 32, :] = jnp.broadcast_to(high, (16, 128)).astype(BF16)


def edge_kernel(image, out):
    rows = image.shape[0]
    row = lax.broadcasted_iota(jnp.int32, (2 * rows, COLS * rows), 0)
    col = lax.broadcasted_iota(jnp.int32, (2 * rows, COLS * rows), 1)
    wanted = jnp.where(row < rows, row * COLS, (row - rows) * COLS + COLS - 1)
    pick = jnp.where(col == wanted, 1.0, 0.0).astype(BF16)
    cells = jnp.concatenate([image[r] for r in range(rows)], axis=1)
    got = dot(pick, cells, NT).astype(BF16)
    out[0] = got[:rows]
    out[1] = got[rows:]


def whole(shape):
    return pl.BlockSpec(shape, lambda k: (0,) * len(shape))


def vm(limit):
    return pltpu.CompilerParams(vmem_limit_bytes=limit << 20, dimension_semantics=("arbitrary",))


BLOCK = pl.BlockSpec((32, 1, 48, 128), lambda k: (0, k, 0, 0))
ATTEND_SCRATCH = [
    pltpu.VMEM((D, D), BF16),
    pltpu.VMEM((D, D), BF16),
    pltpu.VMEM((D, D), BF16),
    pltpu.VMEM((D, D), BF16),
]


def call_edge(image):
    rows = image.shape[0]
    return pl.pallas_call(
        edge_kernel,
        out_shape=jax.ShapeDtypeStruct((2, rows, D), BF16),
        compiler_params=pltpu.CompilerParams(vmem_limit_bytes=32 << 20),
        cost_estimate=pl.CostEstimate(flops=4000000, bytes_accessed=1600000, transcendentals=0),
        name="edge",
    )(image)


def call_pack(image, left, right):
    shape = jax.ShapeDtypeStruct((D + 64, COLS), BF16)
    rows = image.shape[0]
    return pl.pallas_call(
        pack_kernel,
        grid=(1,),
        in_specs=[
            pl.BlockSpec((1, D, COLS), lambda k: (rows - 1, 0, 0)),
            pl.BlockSpec((1, D, COLS), lambda k: (0, 0, 0)),
            whole(left.shape),
            whole(right.shape),
        ],
        out_specs=(whole(shape.shape), whole(shape.shape)),
        out_shape=(shape, shape),
        compiler_params=pltpu.CompilerParams(vmem_limit_bytes=32 << 20),
        cost_estimate=pl.CostEstimate(flops=40000, bytes_accessed=200000, transcendentals=0),
        name="pack",
    )(image, image, left, right)


def call_first(edge, image, halos, weights):
    chunks = 2
    total = image.shape[0]

    def chunk(k):
        return 3 - 3 * k if edge else 1 + k

    rows = pl.BlockSpec((ROWS_CHUNK, D, COLS), lambda k: (chunk(k), 0, 0))
    before = pl.BlockSpec(
        (1, D, COLS), lambda k: (jnp.maximum(chunk(k) * ROWS_CHUNK - 1, 0), 0, 0)
    )
    after = pl.BlockSpec(
        (1, D, COLS), lambda k: (jnp.minimum((chunk(k) + 1) * ROWS_CHUNK, total - 1), 0, 0)
    )
    small = halos + weights
    tokens = chunks * CHUNK
    return pl.pallas_call(
        functools.partial(first_kernel, edge),
        grid=(chunks,),
        in_specs=[rows, before, after] + [whole(a.shape) for a in small],
        out_specs=BLOCK,
        out_shape=jax.ShapeDtypeStruct((32, chunks, 48, 128), BF16),
        scratch_shapes=[
            pltpu.VMEM((ROWS_CHUNK + 2, 160, HID), F32),
            pltpu.VMEM((CHUNK, HID), BF16),
            pltpu.VMEM((9 * COLS, D), BF16),
            pltpu.VMEM((CHUNK, 128), F32),
            pltpu.VMEM((CHUNK, 128), F32),
            pltpu.VMEM((COLS, COLS), BF16),
        ]
        + ATTEND_SCRATCH
        + [
            pltpu.VMEM((HID, D), BF16),
            pltpu.VMEM((TOKENS, HEADS * TOKENS), F32),
            pltpu.VMEM((HEADS, 16, 128), F32),
            pltpu.VMEM((9, HID), F32),
            pltpu.VMEM((2, 48, HID), F32),
        ],
        compiler_params=vm(60 if edge else 48),
        cost_estimate=pl.CostEstimate(
            flops=tokens * 2000000, bytes_accessed=tokens * 800, transcendentals=tokens * 2700
        ),
        name="first",
    )(image, image, image, *small)


def call_grid(one, two, weights):
    chunks = one.shape[1] + two.shape[1]
    tokens = chunks * CHUNK
    shape = (32, 1, 48, 128)
    return pl.pallas_call(
        grid_kernel,
        grid=(chunks,),
        in_specs=[
            pl.BlockSpec(shape, lambda k: (0, jnp.minimum(k, 1), 0, 0)),
            pl.BlockSpec(shape, lambda k: (0, jnp.maximum(k - 2, 0), 0, 0)),
        ]
        + [whole(a.shape) for a in weights],
        out_specs=BLOCK,
        out_shape=jax.ShapeDtypeStruct((32, chunks, 48, 128), BF16),
        scratch_shapes=[pltpu.VMEM((CHUNK, 128), F32), pltpu.VMEM((CHUNK, 128), F32)]
        + ATTEND_SCRATCH
        + [pltpu.VMEM((TOKENS, HEADS * TOKENS), F32), pltpu.VMEM((HEADS, 16, 128), F32)],
        compiler_params=vm(48),
        cost_estimate=pl.CostEstimate(
            flops=tokens * 1000000, bytes_accessed=tokens * 800, transcendentals=tokens * 400
        ),
        name="grid",
    )(one, two, *weights)


def call_last(returned, w_in, w_back):
    chunks = returned.shape[1]
    tokens = chunks * CHUNK
    return pl.pallas_call(
        last_kernel,
        grid=(chunks,),
        in_specs=[BLOCK, whole(w_in.shape), whole(w_back.shape)],
        out_specs=pl.BlockSpec((ROWS_CHUNK, D, COLS), lambda k: (lax.rem(k + 1, chunks), 0, 0)),
        out_shape=jax.ShapeDtypeStruct((chunks * ROWS_CHUNK, D, COLS), BF16),
        scratch_shapes=[pltpu.VMEM((HID, D), BF16)],
        compiler_params=vm(48),
        cost_estimate=pl.CostEstimate(
            flops=tokens * 1000000, bytes_accessed=tokens * 800, transcendentals=tokens * 800
        ),
        name="last",
    )(returned, w_in, w_back)


def shift(x, axis, count, step):
    if step > 0:
        pairs = [(i, i + 1) for i in range(count - 1)]
    else:
        pairs = [(i + 1, i) for i in range(count - 1)]
    return lax.ppermute(x, axis, pairs)


ROW_AXES = ("y", "zh", "zl", "xl")
COL_AXES = ("xh", "core")
GROUP = ("y", "zh", "xh", "core")


def body(
    image, w_expand, dw_kernel, w_project, block_qkv, block_out, block_bias, mlp_in, mlp_out,
    grid_qkv, grid_out, grid_bias, mlp2_in, mlp2_out,
):
    edges = call_edge(image)
    left = shift(edges[1], COL_AXES, 4, 1)
    right = shift(edges[0], COL_AXES, 4, -1)
    down, up = call_pack(image, left, right)
    top = shift(down, ROW_AXES, 32, 1)
    bottom = shift(up, ROW_AXES, 32, -1)
    weights = [
        w_expand, dw_kernel, w_project, block_qkv, block_out, block_bias, mlp_in, mlp_out
    ]
    inner = call_first(False, image, [down, up, left, right], weights)
    inner, top, bottom = lax.optimization_barrier((inner, top, bottom))
    one = lax.all_to_all(inner, GROUP, 0, 0, tiled=True)
    outer = call_first(True, image, [top, bottom, left, right], weights)
    two = lax.all_to_all(outer, GROUP, 0, 0, tiled=True)
    mixed = call_grid(one, two, [grid_qkv, grid_out, grid_bias])
    back = lax.all_to_all(mixed, GROUP, 0, 0, tiled=True)
    return call_last(back, mlp2_in, mlp2_out)


def solution(mesh):
    names = ("y", "zh", "zl", "xl", "xh", "core")
    fine = Mesh(mesh.devices.reshape(4, 2, 2, 2, 2, 2), names)
    spec = P(ROW_AXES, None, COL_AXES)
    return jax.shard_map(
        body, mesh=fine, in_specs=(spec,) + (P(),) * 13, out_specs=spec, check_vma=False
    )
```

```python
import functools
import math

import jax
import jax.numpy as jnp
from jax import lax
from jax.experimental import pallas as pl
from jax.experimental.pallas import tpu as pltpu
from jax.sharding import Mesh, PartitionSpec as P

WIN = 8
D = 192
HID = 768
HEADS = 6
SIZE = 32
COLS = 128
TOKENS = 64
CHUNK = 1024
ROWS_CHUNK = 8
TILES = 16
LAG = 3
LOG2E = 1.4426950408889634
F32 = jnp.float32
BF16 = jnp.bfloat16
NN = (((1,), (0,)), ((), ()))
NT = (((1,), (1,)), ((), ()))
TN = (((0,), (0,)), ((), ()))
C0 = math.sqrt(2.0 / math.pi)
C1 = 0.044715 * C0


def dot(a, b, dims=NN):
    return lax.dot_general(a, b, dims, preferred_element_type=F32)


def gelu(x):
    x = x.astype(BF16)
    inner = x * (BF16(C0) + BF16(C1) * (x * x))
    half = BF16(0.5) * x
    return half + half * jnp.tanh(inner)


def norm(s):
    centre = s - jnp.mean(s, axis=0, keepdims=True)
    spread = jnp.mean(centre * centre, axis=0, keepdims=True)
    return (centre * lax.rsqrt(spread + 1e-05)).astype(BF16)


def mlp(s, w_in_t, w_out):
    return s + dot(w_out, gelu(dot(w_in_t, norm(s))))


def softmax_keys(scores):
    top = jnp.max(scores, axis=0, keepdims=True)
    weights = jnp.exp2(scores - top)
    total = jnp.sum(weights, axis=0, keepdims=True)
    return (weights * (1.0 / total)).astype(BF16)


def attend(s, wq_t, wk, wv_t, w_out_t, bias):
    n = norm(s)
    q = dot(wq_t, n) * (SIZE**-0.5 * LOG2E)
    v = dot(wv_t, n).astype(BF16)
    k = dot(n, wk, TN).astype(BF16)
    left = lax.broadcasted_iota(jnp.int32, (1, 128), 1) < TOKENS
    keep = (lax.broadcasted_iota(jnp.int32, (TOKENS, 1), 0) < SIZE) == left
    zero = jnp.zeros((TOKENS, 128), BF16)
    tiles = s.shape[1] // 128
    ready = {}
    mixed = []

    def score(t):
        here = q[:, 128 * t : 128 * t + 128]
        swapped = pltpu.roll(here, TOKENS, 1).astype(BF16)
        here = here.astype(BF16)
        got = []
        for g in range(2):
            both = jnp.where(left, here, swapped) if g == 0 else jnp.where(left, swapped, here)
            keys = k[(2 * t + g) * TOKENS : (2 * t + g + 1) * TOKENS]
            b = [jnp.where(keep, both[64 * p : 64 * p + 64], zero) for p in range(3)]
            four = jnp.concatenate(
                [jnp.concatenate([b[0], zero], axis=1), jnp.concatenate([zero, b[1]], axis=1)],
                axis=0,
            )
            first = softmax_keys(dot(keys[:, :128], four) + bias[:, :256])
            last = softmax_keys(dot(keys[:, 128:], b[2]) + bias[:, 256:])
            got.append((first[:, :128], first[:, 128:], last))
        ready[t] = got

    def mix(t):
        got = ready.pop(t)
        values = v[:, 128 * t : 128 * t + 128]
        rows = []
        for p in range(3):
            pair = jnp.concatenate(
                [
                    jnp.concatenate([got[0][p], zero], axis=1),
                    jnp.concatenate([zero, got[1][p]], axis=1),
                ],
                axis=0,
            )
            out = dot(values[64 * p : 64 * p + 64], pair)
            a, b = out[:, :128], out[:, 128:]
            rows.append(jnp.where(left, a[:SIZE], pltpu.roll(b[:SIZE], TOKENS, 1)))
            rows.append(jnp.where(left, pltpu.roll(a[SIZE:], TOKENS, 1), b[SIZE:]))
        mixed.append(jnp.concatenate(rows, axis=0).astype(BF16))

    for t in range(tiles + LAG):
        if t < tiles:
            score(t)
        if t >= LAG:
            mix(t - LAG)
    return s + dot(w_out_t, jnp.concatenate(mixed, axis=1))


def bias_rows(table, padded, bias):
    lane = lax.broadcasted_iota(jnp.int32, (16, 128), 1)
    line = lax.broadcasted_iota(jnp.int32, (16, 128), 0)
    spread = jnp.where(lane // WIN == line, 1.0, 0.0)
    left = lax.broadcasted_iota(jnp.int32, (WIN, 128), 1) < TOKENS
    padded[...] = jnp.zeros_like(padded)
    heads = []
    for h in range(HEADS):
        padded[h, 0:15, 0:15] = table[h]
        cells = lax.dot_general(
            padded[h][:, :16], spread, TN, precision=lax.Precision.HIGHEST,
            preferred_element_type=F32,
        )
        rows = [
            jnp.sum(jnp.where(line == 7 - v + lane % WIN, cells, 0.0), axis=0, keepdims=True)
            for v in range(WIN)
        ]
        heads.append(jnp.concatenate(rows, axis=0))
    for u in range(WIN):
        for p in range(3):
            start = (7 - u) * WIN
            even = pltpu.roll(heads[2 * p], (128 - start) % 128, 1)
            odd = pltpu.roll(heads[2 * p + 1], (64 - start) % 128, 1)
            bias[u * WIN : (u + 1) * WIN, 128 * p : 128 * p + 128] = (
                jnp.where(left, even, odd) * LOG2E
            )


def prepare(w_qkv, w_out, table, wq_t, wk, wv_t, w_out_t, bias, padded):
    wq_t[...] = w_qkv[:, 0:D].T
    wk[...] = w_qkv[:, D : 2 * D]
    wv_t[...] = w_qkv[:, 2 * D : 3 * D].T
    w_out_t[...] = w_out[...].T
    bias_rows(table, padded, bias)


def gather_groups(lo, hi):
    parts = []
    for g in range(TILES):
        at = pl.ds(g, TOKENS, stride=TILES)
        parts.append(jnp.concatenate([lo[at, :], hi[at, :][:, :64]], axis=1))
    return jnp.concatenate(parts, axis=0).T


def first_kernel(
    edge, image, before, after, top, bottom, left, right,
    w_expand, taps, w_project, w_qkv, w_out, table, w_in, w_back,
    out, expanded, mobile, tokens, lo, hi, place, wq_t, wk, wv_t, w_out_t, w_in_t, bias, padded,
    dw, side,
):
    step = pl.program_id(0)
    line = lax.broadcasted_iota(jnp.int32, (16, HID), 0)

    def laid(x):
        return dot(place[...], x, NT).astype(BF16)

    def expand(x, sides, rows):
        cells = gelu(dot(x, w_expand[...])).astype(F32)
        for i, r in enumerate(rows):
            e = cells[COLS * i : COLS * (i + 1)]
            expanded[r, 16:144, :] = e
            prev = pltpu.roll(e[112:128], 1, 0)
            expanded[r, 0:16, :] = jnp.where(line == 0, sides[0][r : r + 1], prev)
            follow = pltpu.roll(e[0:16], 15, 0)
            expanded[r, 144:160, :] = jnp.where(line == 15, sides[1][r : r + 1], follow)

    @pl.when(step == 0)
    def _():
        for i in range(3):
            dw[3 * i : 3 * i + 3, :] = taps[i].astype(F32)
        for i, halo in enumerate((left, right)):
            side[i, 8:40, :] = gelu(dot(halo[...], w_expand[...])).astype(F32)
            if edge:
                for j, message in enumerate((top, bottom)):
                    pair = message[D + 32 * i : D + 32 * i + 32, :]
                    corner = jnp.concatenate([pair[0:16], pair[16:32, 0:64]], axis=1)
                    ends = gelu(dot(corner, w_expand[...])).astype(F32)
                    side[i, 40 * j : 40 * j + 8, :] = jnp.broadcast_to(ends[0:1], (8, HID))
        prepare(w_qkv, w_out, table, wq_t, wk, wv_t, w_out_t, bias, padded)
        w_in_t[...] = w_in[...].T
        row = lax.broadcasted_iota(jnp.int32, (COLS, COLS), 0)
        col = lax.broadcasted_iota(jnp.int32, (COLS, COLS), 1)
        place[...] = jnp.where(col == (row % 16) * 8 + row // 16, 1.0, 0.0).astype(BF16)

    order = (step + 1) if not edge else jnp.where(step == 0, 3, 0)
    start = pl.multiple_of(order * ROWS_CHUNK, 8)
    sides = [side[i, pl.ds(start, 24), :][7:23] for i in range(2)]

    def begin():
        above = before[0]
        if edge:
            above = jnp.where(step == 0, above, top[0:D, :])
        pair = jnp.concatenate([laid(above), laid(image[0])], axis=0)
        tokens[0:COLS, :] = pair[COLS:]
        expand(pair, sides, (0, 1))

    below = after[0]
    if edge:
        below = jnp.where(step == 0, bottom[0:D, :], below)
        begin()
    else:
        pl.when(step == 0)(begin)

        @pl.when(step > 0)
        def _():
            tokens[0:COLS, :] = tokens[8 * COLS : 9 * COLS, :]
            expanded[0:2] = expanded[8:10]

    for r in range(1, ROWS_CHUNK):
        tokens[COLS * r : COLS * (r + 1), :] = laid(image[r])
    tokens[COLS * 8 : COLS * 9, :] = laid(below)
    for half in range(2):
        x = tokens[COLS * (1 + 4 * half) : COLS * (5 + 4 * half), :]
        expand(x, sides, range(2 + 4 * half, 6 + 4 * half))

    for r in range(ROWS_CHUNK):
        for block in range(HID // 128):
            lanes = slice(block * 128, (block + 1) * 128)
            conv = None
            for i in range(3):
                for k in range(3):
                    term = expanded[r + i, 16 * k : 16 * k + COLS, lanes] * dw[
                        3 * i + k : 3 * i + k + 1, lanes
                    ]
                    conv = term if conv is None else conv + term
            mobile[COLS * r : COLS * (r + 1), lanes] = gelu(conv)

    s = tokens[0:CHUNK, :].astype(F32) + dot(mobile[...], w_project[...], NT)
    lo[...] = s[:, :128]
    hi[:, :64] = s[:, 128:]
    s = gather_groups(lo, hi)
    s = attend(s, wq_t[...], wk[...], wv_t[...], w_out_t[...], bias)
    s = mlp(s, w_in_t[...], w_back[...]).T.reshape(TILES, WIN, WIN, D)
    for r in range(ROWS_CHUNK):
        rows = s[:, r].reshape(2, 4, 16, D)
        at = slice(4 * r, 4 * r + 4)
        out[at, 0, 0:16, :] = rows[0, :, :, 0:128].astype(BF16)
        out[at, 0, 16:32, :] = rows[1, :, :, 0:128].astype(BF16)
        out[at, 0, 32:48, :] = jnp.concatenate(
            [rows[0, :, :, 128:], rows[1, :, :, 128:]], axis=-1
        ).astype(BF16)


def grid_kernel(inp, w_qkv, w_out, table, *rest):
    out, lo, hi, wq_t, wk, wv_t, w_out_t, bias, padded = rest[-9:]

    @pl.when(pl.program_id(0) == 0)
    def _():
        prepare(w_qkv, w_out, table, wq_t, wk, wv_t, w_out_t, bias, padded)

    for src in range(32):
        lo[32 * src : 32 * src + 32, :] = inp[src, 0, 0:32, :].astype(F32)
        both = inp[src, 0, 32:48, :].astype(F32)
        hi[32 * src : 32 * src + 16, :] = both
        hi[32 * src + 16 : 32 * src + 32, :] = pltpu.roll(both, 64, 1)
    s = gather_groups(lo, hi)
    s = attend(s, wq_t[...], wk[...], wv_t[...], w_out_t[...], bias).T
    for g in range(TILES):
        at = pl.ds(g, TOKENS, stride=TILES)
        rows = s[g * TOKENS : (g + 1) * TOKENS]
        lo[at, :] = rows[:, :128]
        hi[at, :] = jnp.concatenate([rows[:, 128:], rows[:, 128:]], axis=1)
    left = lax.broadcasted_iota(jnp.int32, (16, 128), 1) < 64
    for src in range(32):
        out[src, 0, 0:32, :] = lo[32 * src : 32 * src + 32, :].astype(BF16)
        out[src, 0, 32:48, :] = jnp.where(
            left, hi[32 * src : 32 * src + 16, :], hi[32 * src + 16 : 32 * src + 32, :]
        ).astype(BF16)


def last_kernel(inp, w_in, w_back, out, w_in_t):
    @pl.when(pl.program_id(0) == 0)
    def _():
        w_in_t[...] = w_in[...].T

    rows = []
    for r in range(ROWS_CHUNK):
        got = inp[4 * r : 4 * r + 4, 0].astype(F32)
        both = got[:, 32:48].reshape(64, 128)
        for i in range(2):
            low = got[:, 16 * i : 16 * i + 16].reshape(64, 128)
            rows.append(jnp.concatenate([low, both[:, 64 * i : 64 * i + 64]], axis=1))
    s = jnp.concatenate(rows, axis=0).T
    s = mlp(s, w_in_t[...], w_back[...]).astype(BF16)
    for r in range(ROWS_CHUNK):
        out[r] = s[:, COLS * r : COLS * (r + 1)]


def pack_kernel(lowest, highest, left, right, down, up):
    for r, cells, out in ((left.shape[0] - 1, lowest, down), (0, highest, up)):
        out[0:D, :] = cells[0]
        for i, halo in enumerate((left, right)):
            cell = halo[r : r + 1, :].astype(F32)
            high = jnp.concatenate([cell[:, 128:], cell[:, 128:]], axis=1)
            at = D + 32 * i
            out[at : at + 16, :] = jnp.broadcast_to(cell[:, :128], (16, 128)).astype(BF16)
            out[at + 16 : at + 32, :] = jnp.broadcast_to(high, (16, 128)).astype(BF16)


def edge_kernel(image, out):
    rows = image.shape[0]
    row = lax.broadcasted_iota(jnp.int32, (2 * rows, COLS * rows), 0)
    col = lax.broadcasted_iota(jnp.int32, (2 * rows, COLS * rows), 1)
    wanted = jnp.where(row < rows, row * COLS, (row - rows) * COLS + COLS - 1)
    pick = jnp.where(col == wanted, 1.0, 0.0).astype(BF16)
    cells = jnp.concatenate([image[r] for r in range(rows)], axis=1)
    got = dot(pick, cells, NT).astype(BF16)
    out[0] = got[:rows]
    out[1] = got[rows:]


def whole(shape):
    return pl.BlockSpec(shape, lambda k: (0,) * len(shape))


def vm(limit):
    return pltpu.CompilerParams(vmem_limit_bytes=limit << 20, dimension_semantics=("arbitrary",))


BLOCK = pl.BlockSpec((32, 1, 48, 128), lambda k: (0, k, 0, 0))
ATTEND_SCRATCH = [
    pltpu.VMEM((D, D), BF16),
    pltpu.VMEM((D, D), BF16),
    pltpu.VMEM((D, D), BF16),
    pltpu.VMEM((D, D), BF16),
]


def call_edge(image):
    rows = image.shape[0]
    return pl.pallas_call(
        edge_kernel,
        out_shape=jax.ShapeDtypeStruct((2, rows, D), BF16),
        compiler_params=pltpu.CompilerParams(vmem_limit_bytes=32 << 20),
        cost_estimate=pl.CostEstimate(flops=4000000, bytes_accessed=1600000, transcendentals=0),
        name="edge",
    )(image)


def call_pack(image, left, right):
    shape = jax.ShapeDtypeStruct((D + 64, COLS), BF16)
    rows = image.shape[0]
    return pl.pallas_call(
        pack_kernel,
        grid=(1,),
        in_specs=[
            pl.BlockSpec((1, D, COLS), lambda k: (rows - 1, 0, 0)),
            pl.BlockSpec((1, D, COLS), lambda k: (0, 0, 0)),
            whole(left.shape),
            whole(right.shape),
        ],
        out_specs=(whole(shape.shape), whole(shape.shape)),
        out_shape=(shape, shape),
        compiler_params=pltpu.CompilerParams(vmem_limit_bytes=32 << 20),
        cost_estimate=pl.CostEstimate(flops=40000, bytes_accessed=200000, transcendentals=0),
        name="pack",
    )(image, image, left, right)


def call_first(edge, image, halos, weights):
    chunks = 2
    total = image.shape[0]

    def chunk(k):
        return 3 - 3 * k if edge else 1 + k

    rows = pl.BlockSpec((ROWS_CHUNK, D, COLS), lambda k: (chunk(k), 0, 0))
    before = pl.BlockSpec(
        (1, D, COLS), lambda k: (jnp.maximum(chunk(k) * ROWS_CHUNK - 1, 0), 0, 0)
    )
    after = pl.BlockSpec(
        (1, D, COLS), lambda k: (jnp.minimum((chunk(k) + 1) * ROWS_CHUNK, total - 1), 0, 0)
    )
    small = halos + weights
    tokens = chunks * CHUNK
    return pl.pallas_call(
        functools.partial(first_kernel, edge),
        grid=(chunks,),
        in_specs=[rows, before, after] + [whole(a.shape) for a in small],
        out_specs=BLOCK,
        out_shape=jax.ShapeDtypeStruct((32, chunks, 48, 128), BF16),
        scratch_shapes=[
            pltpu.VMEM((ROWS_CHUNK + 2, 160, HID), F32),
            pltpu.VMEM((CHUNK, HID), BF16),
            pltpu.VMEM((9 * COLS, D), BF16),
            pltpu.VMEM((CHUNK, 128), F32),
            pltpu.VMEM((CHUNK, 128), F32),
            pltpu.VMEM((COLS, COLS), BF16),
        ]
        + ATTEND_SCRATCH
        + [
            pltpu.VMEM((HID, D), BF16),
            pltpu.VMEM((TOKENS, HEADS * TOKENS), F32),
            pltpu.VMEM((HEADS, 16, 128), F32),
            pltpu.VMEM((9, HID), F32),
            pltpu.VMEM((2, 48, HID), F32),
        ],
        compiler_params=vm(60 if edge else 48),
        cost_estimate=pl.CostEstimate(
            flops=tokens * 2000000, bytes_accessed=tokens * 800, transcendentals=tokens * 2700
        ),
        name="first",
    )(image, image, image, *small)


def call_grid(base, total, arrived, weights, earlier):
    chunks = arrived.shape[1]
    tokens = chunks * CHUNK
    operands = [arrived] + weights
    specs = [BLOCK] + [whole(a.shape) for a in weights]
    aliases = {}
    if earlier is not None:
        aliases = {len(operands): 0}
        operands.append(earlier)
        specs.append(pl.BlockSpec(memory_space=pl.ANY))
    return pl.pallas_call(
        grid_kernel,
        grid=(chunks,),
        in_specs=specs,
        out_specs=pl.BlockSpec((32, 1, 48, 128), lambda k: (0, base + k, 0, 0)),
        out_shape=jax.ShapeDtypeStruct((32, total, 48, 128), BF16),
        scratch_shapes=[pltpu.VMEM((CHUNK, 128), F32), pltpu.VMEM((CHUNK, 128), F32)]
        + ATTEND_SCRATCH
        + [pltpu.VMEM((TOKENS, HEADS * TOKENS), F32), pltpu.VMEM((HEADS, 16, 128), F32)],
        input_output_aliases=aliases,
        compiler_params=vm(48),
        cost_estimate=pl.CostEstimate(
            flops=tokens * 1000000, bytes_accessed=tokens * 800, transcendentals=tokens * 400
        ),
        name="grid",
    )(*operands)


def call_last(returned, w_in, w_back):
    chunks = returned.shape[1]
    tokens = chunks * CHUNK
    return pl.pallas_call(
        last_kernel,
        grid=(chunks,),
        in_specs=[BLOCK, whole(w_in.shape), whole(w_back.shape)],
        out_specs=pl.BlockSpec((ROWS_CHUNK, D, COLS), lambda k: (lax.rem(k + 1, chunks), 0, 0)),
        out_shape=jax.ShapeDtypeStruct((chunks * ROWS_CHUNK, D, COLS), BF16),
        scratch_shapes=[pltpu.VMEM((HID, D), BF16)],
        compiler_params=vm(48),
        cost_estimate=pl.CostEstimate(
            flops=tokens * 1000000, bytes_accessed=tokens * 800, transcendentals=tokens * 800
        ),
        name="last",
    )(returned, w_in, w_back)


def shift(x, axis, count, step):
    if step > 0:
        pairs = [(i, i + 1) for i in range(count - 1)]
    else:
        pairs = [(i + 1, i) for i in range(count - 1)]
    return lax.ppermute(x, axis, pairs)


ROW_AXES = ("y", "zh", "zl", "xl")
COL_AXES = ("xh", "core")
GROUP = ("y", "zh", "xh", "core")


def body(
    image, w_expand, dw_kernel, w_project, block_qkv, block_out, block_bias, mlp_in, mlp_out,
    grid_qkv, grid_out, grid_bias, mlp2_in, mlp2_out,
):
    edges = call_edge(image)
    left = shift(edges[1], COL_AXES, 4, 1)
    right = shift(edges[0], COL_AXES, 4, -1)
    down, up = call_pack(image, left, right)
    top = shift(down, ROW_AXES, 32, 1)
    bottom = shift(up, ROW_AXES, 32, -1)
    weights = [
        w_expand, dw_kernel, w_project, block_qkv, block_out, block_bias, mlp_in, mlp_out
    ]
    inner = call_first(False, image, [down, up, left, right], weights)
    inner, top, bottom = lax.optimization_barrier((inner, top, bottom))
    one = lax.all_to_all(inner, GROUP, 0, 0, tiled=True)
    outer = call_first(True, image, [top, bottom, left, right], weights)
    two = lax.all_to_all(outer, GROUP, 0, 0, tiled=True)
    weights = [grid_qkv, grid_out, grid_bias]
    mixed = call_grid(0, 4, one, weights, None)
    mixed = call_grid(2, 4, two, weights, mixed)
    back = lax.all_to_all(mixed, GROUP, 0, 0, tiled=True)
    return call_last(back, mlp2_in, mlp2_out)


def solution(mesh):
    names = ("y", "zh", "zl", "xl", "xh", "core")
    fine = Mesh(mesh.devices.reshape(4, 2, 2, 2, 2, 2), names)
    spec = P(ROW_AXES, None, COL_AXES)
    return jax.shard_map(
        body, mesh=fine, in_specs=(spec,) + (P(),) * 13, out_specs=spec, check_vma=False
    )
```

```python
import functools
import math

import jax
import jax.numpy as jnp
from jax import lax
from jax.experimental import pallas as pl
from jax.experimental.pallas import tpu as pltpu
from jax.sharding import Mesh, PartitionSpec as P

WIN = 8
D = 192
HID = 768
HEADS = 6
SIZE = 32
COLS = 128
TOKENS = 64
CHUNK = 1024
ROWS_CHUNK = 8
TILES = 16
LAG = 3
LOG2E = 1.4426950408889634
F32 = jnp.float32
BF16 = jnp.bfloat16
NN = (((1,), (0,)), ((), ()))
NT = (((1,), (1,)), ((), ()))
TN = (((0,), (0,)), ((), ()))
C0 = math.sqrt(2.0 / math.pi)
C1 = 0.044715 * C0


def dot(a, b, dims=NN):
    return lax.dot_general(a, b, dims, preferred_element_type=F32)


def gelu(x):
    x = x.astype(BF16)
    inner = x * (BF16(C0) + BF16(C1) * (x * x))
    half = BF16(0.5) * x
    return half + half * jnp.tanh(inner)


def norm(s):
    centre = s - jnp.mean(s, axis=0, keepdims=True)
    spread = jnp.mean(centre * centre, axis=0, keepdims=True)
    return (centre * lax.rsqrt(spread + 1e-05)).astype(BF16)


def mlp(s, w_in_t, w_out):
    return s + dot(w_out, gelu(dot(w_in_t, norm(s))))


def softmax_keys(scores):
    top = jnp.max(scores, axis=0, keepdims=True)
    weights = jnp.exp2(scores - top)
    total = jnp.sum(weights, axis=0, keepdims=True)
    return (weights * (1.0 / total)).astype(BF16)


def attend(s, wq_t, wk, wv_t, w_out_t, bias):
    n = norm(s)
    q = dot(wq_t, n) * (SIZE**-0.5 * LOG2E)
    v = dot(wv_t, n).astype(BF16)
    k = dot(n, wk, TN).astype(BF16)
    left = lax.broadcasted_iota(jnp.int32, (1, 128), 1) < TOKENS
    keep = (lax.broadcasted_iota(jnp.int32, (TOKENS, 1), 0) < SIZE) == left
    zero = jnp.zeros((TOKENS, 128), BF16)
    tiles = s.shape[1] // 128
    ready = {}
    mixed = []

    def score(t):
        here = q[:, 128 * t : 128 * t + 128]
        swapped = pltpu.roll(here, TOKENS, 1).astype(BF16)
        here = here.astype(BF16)
        got = []
        for g in range(2):
            both = jnp.where(left, here, swapped) if g == 0 else jnp.where(left, swapped, here)
            keys = k[(2 * t + g) * TOKENS : (2 * t + g + 1) * TOKENS]
            b = [jnp.where(keep, both[64 * p : 64 * p + 64], zero) for p in range(3)]
            four = jnp.concatenate(
                [jnp.concatenate([b[0], zero], axis=1), jnp.concatenate([zero, b[1]], axis=1)],
                axis=0,
            )
            first = softmax_keys(dot(keys[:, :128], four) + bias[:, :256])
            last = softmax_keys(dot(keys[:, 128:], b[2]) + bias[:, 256:])
            got.append((first[:, :128], first[:, 128:], last))
        ready[t] = got

    def mix(t):
        got = ready.pop(t)
        values = v[:, 128 * t : 128 * t + 128]
        rows = []
        for p in range(3):
            pair = jnp.concatenate(
                [
                    jnp.concatenate([got[0][p], zero], axis=1),
                    jnp.concatenate([zero, got[1][p]], axis=1),
                ],
                axis=0,
            )
            out = dot(values[64 * p : 64 * p + 64], pair)
            a, b = out[:, :128], out[:, 128:]
            rows.append(jnp.where(left, a[:SIZE], pltpu.roll(b[:SIZE], TOKENS, 1)))
            rows.append(jnp.where(left, pltpu.roll(a[SIZE:], TOKENS, 1), b[SIZE:]))
        mixed.append(jnp.concatenate(rows, axis=0).astype(BF16))

    for t in range(tiles + LAG):
        if t < tiles:
            score(t)
        if t >= LAG:
            mix(t - LAG)
    return s + dot(w_out_t, jnp.concatenate(mixed, axis=1))


def bias_rows(table, padded, bias):
    lane = lax.broadcasted_iota(jnp.int32, (16, 128), 1)
    line = lax.broadcasted_iota(jnp.int32, (16, 128), 0)
    spread = jnp.where(lane // WIN == line, 1.0, 0.0)
    left = lax.broadcasted_iota(jnp.int32, (WIN, 128), 1) < TOKENS
    padded[...] = jnp.zeros_like(padded)
    heads = []
    for h in range(HEADS):
        padded[h, 0:15, 0:15] = table[h]
        cells = lax.dot_general(
            padded[h][:, :16], spread, TN, precision=lax.Precision.HIGHEST,
            preferred_element_type=F32,
        )
        rows = [
            jnp.sum(jnp.where(line == 7 - v + lane % WIN, cells, 0.0), axis=0, keepdims=True)
            for v in range(WIN)
        ]
        heads.append(jnp.concatenate(rows, axis=0))
    for u in range(WIN):
        for p in range(3):
            start = (7 - u) * WIN
            even = pltpu.roll(heads[2 * p], (128 - start) % 128, 1)
            odd = pltpu.roll(heads[2 * p + 1], (64 - start) % 128, 1)
            bias[u * WIN : (u + 1) * WIN, 128 * p : 128 * p + 128] = (
                jnp.where(left, even, odd) * LOG2E
            )


def prepare(w_qkv, w_out, table, wq_t, wk, wv_t, w_out_t, bias, padded):
    wq_t[...] = w_qkv[:, 0:D].T
    wk[...] = w_qkv[:, D : 2 * D]
    wv_t[...] = w_qkv[:, 2 * D : 3 * D].T
    w_out_t[...] = w_out[...].T
    bias_rows(table, padded, bias)


def gather_groups(lo, hi):
    parts = []
    for g in range(TILES):
        at = pl.ds(g, TOKENS, stride=TILES)
        parts.append(jnp.concatenate([lo[at, :], hi[at, :][:, :64]], axis=1))
    return jnp.concatenate(parts, axis=0).T


def first_kernel(
    edge, image, before, after, top, bottom, left, right,
    w_expand, taps, w_project, w_qkv, w_out, table, w_in, w_back,
    out, expanded, mobile, tokens, lo, hi, place, wq_t, wk, wv_t, w_out_t, w_in_t, bias, padded,
    dw, side,
):
    step = pl.program_id(0)
    line = lax.broadcasted_iota(jnp.int32, (16, HID), 0)

    def laid(x):
        return dot(place[...], x, NT).astype(BF16)

    def expand(x, sides, rows):
        cells = gelu(dot(x, w_expand[...])).astype(F32)
        for i, r in enumerate(rows):
            e = cells[COLS * i : COLS * (i + 1)]
            expanded[r, 16:144, :] = e
            prev = pltpu.roll(e[112:128], 1, 0)
            expanded[r, 0:16, :] = jnp.where(line == 0, sides[0][r : r + 1], prev)
            follow = pltpu.roll(e[0:16], 15, 0)
            expanded[r, 144:160, :] = jnp.where(line == 15, sides[1][r : r + 1], follow)

    @pl.when(step == 0)
    def _():
        for i in range(3):
            dw[3 * i : 3 * i + 3, :] = taps[i].astype(F32)
        for i, halo in enumerate((left, right)):
            side[i, 8:40, :] = gelu(dot(halo[...], w_expand[...])).astype(F32)
            if edge:
                for j, message in enumerate((top, bottom)):
                    pair = message[D + 32 * i : D + 32 * i + 32, :]
                    corner = jnp.concatenate([pair[0:16], pair[16:32, 0:64]], axis=1)
                    ends = gelu(dot(corner, w_expand[...])).astype(F32)
                    side[i, 40 * j : 40 * j + 8, :] = jnp.broadcast_to(ends[0:1], (8, HID))
        prepare(w_qkv, w_out, table, wq_t, wk, wv_t, w_out_t, bias, padded)
        w_in_t[...] = w_in[...].T
        row = lax.broadcasted_iota(jnp.int32, (COLS, COLS), 0)
        col = lax.broadcasted_iota(jnp.int32, (COLS, COLS), 1)
        place[...] = jnp.where(col == (row % 16) * 8 + row // 16, 1.0, 0.0).astype(BF16)

    order = (step + 1) if not edge else jnp.where(step == 0, 3, 0)
    start = pl.multiple_of(order * ROWS_CHUNK, 8)
    sides = [side[i, pl.ds(start, 24), :][7:23] for i in range(2)]

    def begin():
        above = before[0]
        if edge:
            above = jnp.where(step == 0, above, top[0:D, :])
        pair = jnp.concatenate([laid(above), laid(image[0])], axis=0)
        tokens[0:COLS, :] = pair[COLS:]
        expand(pair, sides, (0, 1))

    below = after[0]
    if edge:
        below = jnp.where(step == 0, bottom[0:D, :], below)
        begin()
    else:
        pl.when(step == 0)(begin)

        @pl.when(step > 0)
        def _():
            tokens[0:COLS, :] = tokens[8 * COLS : 9 * COLS, :]
            expanded[0:2] = expanded[8:10]

    for r in range(1, ROWS_CHUNK):
        tokens[COLS * r : COLS * (r + 1), :] = laid(image[r])
    tokens[COLS * 8 : COLS * 9, :] = laid(below)
    for half in range(2):
        x = tokens[COLS * (1 + 4 * half) : COLS * (5 + 4 * half), :]
        expand(x, sides, range(2 + 4 * half, 6 + 4 * half))

    for r in range(ROWS_CHUNK):
        for block in range(HID // 128):
            lanes = slice(block * 128, (block + 1) * 128)
            conv = None
            for i in range(3):
                for k in range(3):
                    term = expanded[r + i, 16 * k : 16 * k + COLS, lanes] * dw[
                        3 * i + k : 3 * i + k + 1, lanes
                    ]
                    conv = term if conv is None else conv + term
            mobile[COLS * r : COLS * (r + 1), lanes] = gelu(conv)

    s = tokens[0:CHUNK, :].astype(F32) + dot(mobile[...], w_project[...], NT)
    lo[...] = s[:, :128]
    hi[:, :64] = s[:, 128:]
    s = gather_groups(lo, hi)
    s = attend(s, wq_t[...], wk[...], wv_t[...], w_out_t[...], bias)
    s = mlp(s, w_in_t[...], w_back[...]).T.reshape(TILES, WIN, WIN, D)
    for r in range(ROWS_CHUNK):
        rows = s[:, r].reshape(2, 4, 16, D)
        at = slice(4 * r, 4 * r + 4)
        out[at, 0, 0:16, :] = rows[0, :, :, 0:128].astype(BF16)
        out[at, 0, 16:32, :] = rows[1, :, :, 0:128].astype(BF16)
        out[at, 0, 32:48, :] = jnp.concatenate(
            [rows[0, :, :, 128:], rows[1, :, :, 128:]], axis=-1
        ).astype(BF16)


def grid_kernel(inp, w_qkv, w_out, table, *rest):
    out, lo, hi, wq_t, wk, wv_t, w_out_t, bias, padded = rest[-9:]

    @pl.when(pl.program_id(0) == 0)
    def _():
        prepare(w_qkv, w_out, table, wq_t, wk, wv_t, w_out_t, bias, padded)

    for src in range(32):
        lo[32 * src : 32 * src + 32, :] = inp[src, 0, 0:32, :].astype(F32)
        both = inp[src, 0, 32:48, :].astype(F32)
        hi[32 * src : 32 * src + 16, :] = both
        hi[32 * src + 16 : 32 * src + 32, :] = pltpu.roll(both, 64, 1)
    s = gather_groups(lo, hi)
    s = attend(s, wq_t[...], wk[...], wv_t[...], w_out_t[...], bias).T
    for g in range(TILES):
        at = pl.ds(g, TOKENS, stride=TILES)
        rows = s[g * TOKENS : (g + 1) * TOKENS]
        lo[at, :] = rows[:, :128]
        hi[at, :] = jnp.concatenate([rows[:, 128:], rows[:, 128:]], axis=1)
    left = lax.broadcasted_iota(jnp.int32, (16, 128), 1) < 64
    for src in range(32):
        out[src, 0, 0:32, :] = lo[32 * src : 32 * src + 32, :].astype(BF16)
        out[src, 0, 32:48, :] = jnp.where(
            left, hi[32 * src : 32 * src + 16, :], hi[32 * src + 16 : 32 * src + 32, :]
        ).astype(BF16)


def last_kernel(inp, w_in, w_back, out, w_in_t):
    @pl.when(pl.program_id(0) == 0)
    def _():
        w_in_t[...] = w_in[...].T

    rows = []
    for r in range(ROWS_CHUNK):
        got = inp[4 * r : 4 * r + 4, 0].astype(F32)
        both = got[:, 32:48].reshape(64, 128)
        for i in range(2):
            low = got[:, 16 * i : 16 * i + 16].reshape(64, 128)
            rows.append(jnp.concatenate([low, both[:, 64 * i : 64 * i + 64]], axis=1))
    s = jnp.concatenate(rows, axis=0).T
    s = mlp(s, w_in_t[...], w_back[...]).astype(BF16)
    for r in range(ROWS_CHUNK):
        out[r] = s[:, COLS * r : COLS * (r + 1)]


def pack_kernel(lowest, highest, left, right, down, up):
    for r, cells, out in ((left.shape[0] - 1, lowest, down), (0, highest, up)):
        out[0:D, :] = cells[0]
        for i, halo in enumerate((left, right)):
            cell = halo[r : r + 1, :].astype(F32)
            high = jnp.concatenate([cell[:, 128:], cell[:, 128:]], axis=1)
            at = D + 32 * i
            out[at : at + 16, :] = jnp.broadcast_to(cell[:, :128], (16, 128)).astype(BF16)
            out[at + 16 : at + 32, :] = jnp.broadcast_to(high, (16, 128)).astype(BF16)


def edge_kernel(image, out):
    rows = image.shape[0]
    row = lax.broadcasted_iota(jnp.int32, (2 * rows, COLS * rows), 0)
    col = lax.broadcasted_iota(jnp.int32, (2 * rows, COLS * rows), 1)
    wanted = jnp.where(row < rows, row * COLS, (row - rows) * COLS + COLS - 1)
    pick = jnp.where(col == wanted, 1.0, 0.0).astype(BF16)
    cells = jnp.concatenate([image[r] for r in range(rows)], axis=1)
    got = dot(pick, cells, NT).astype(BF16)
    out[0] = got[:rows]
    out[1] = got[rows:]


def whole(shape):
    return pl.BlockSpec(shape, lambda k: (0,) * len(shape))


def vm(limit):
    return pltpu.CompilerParams(vmem_limit_bytes=limit << 20, dimension_semantics=("arbitrary",))


BLOCK = pl.BlockSpec((32, 1, 48, 128), lambda k: (0, k, 0, 0))
ATTEND_SCRATCH = [
    pltpu.VMEM((D, D), BF16),
    pltpu.VMEM((D, D), BF16),
    pltpu.VMEM((D, D), BF16),
    pltpu.VMEM((D, D), BF16),
]


def call_edge(image):
    rows = image.shape[0]
    return pl.pallas_call(
        edge_kernel,
        out_shape=jax.ShapeDtypeStruct((2, rows, D), BF16),
        compiler_params=pltpu.CompilerParams(vmem_limit_bytes=32 << 20),
        cost_estimate=pl.CostEstimate(flops=4000000, bytes_accessed=1600000, transcendentals=0),
        name="edge",
    )(image)


def call_pack(image, left, right):
    shape = jax.ShapeDtypeStruct((D + 64, COLS), BF16)
    rows = image.shape[0]
    return pl.pallas_call(
        pack_kernel,
        grid=(1,),
        in_specs=[
            pl.BlockSpec((1, D, COLS), lambda k: (rows - 1, 0, 0)),
            pl.BlockSpec((1, D, COLS), lambda k: (0, 0, 0)),
            whole(left.shape),
            whole(right.shape),
        ],
        out_specs=(whole(shape.shape), whole(shape.shape)),
        out_shape=(shape, shape),
        compiler_params=pltpu.CompilerParams(vmem_limit_bytes=32 << 20),
        cost_estimate=pl.CostEstimate(flops=40000, bytes_accessed=200000, transcendentals=0),
        name="pack",
    )(image, image, left, right)


def call_first(edge, image, halos, weights):
    chunks = 2
    total = image.shape[0]

    def chunk(k):
        return 3 - 3 * k if edge else 1 + k

    rows = pl.BlockSpec((ROWS_CHUNK, D, COLS), lambda k: (chunk(k), 0, 0))
    before = pl.BlockSpec(
        (1, D, COLS), lambda k: (jnp.maximum(chunk(k) * ROWS_CHUNK - 1, 0), 0, 0)
    )
    after = pl.BlockSpec(
        (1, D, COLS), lambda k: (jnp.minimum((chunk(k) + 1) * ROWS_CHUNK, total - 1), 0, 0)
    )
    small = halos + weights
    tokens = chunks * CHUNK
    return pl.pallas_call(
        functools.partial(first_kernel, edge),
        grid=(chunks,),
        in_specs=[rows, before, after] + [whole(a.shape) for a in small],
        out_specs=BLOCK,
        out_shape=jax.ShapeDtypeStruct((32, chunks, 48, 128), BF16),
        scratch_shapes=[
            pltpu.VMEM((ROWS_CHUNK + 2, 160, HID), F32),
            pltpu.VMEM((CHUNK, HID), BF16),
            pltpu.VMEM((9 * COLS, D), BF16),
            pltpu.VMEM((CHUNK, 128), F32),
            pltpu.VMEM((CHUNK, 128), F32),
            pltpu.VMEM((COLS, COLS), BF16),
        ]
        + ATTEND_SCRATCH
        + [
            pltpu.VMEM((HID, D), BF16),
            pltpu.VMEM((TOKENS, HEADS * TOKENS), F32),
            pltpu.VMEM((HEADS, 16, 128), F32),
            pltpu.VMEM((9, HID), F32),
            pltpu.VMEM((2, 48, HID), F32),
        ],
        compiler_params=vm(60 if edge else 48),
        cost_estimate=pl.CostEstimate(
            flops=tokens * 2000000, bytes_accessed=tokens * 800, transcendentals=tokens * 2700
        ),
        name="first",
    )(image, image, image, *small)


def call_grid(base, total, arrived, weights, earlier):
    chunks = arrived.shape[1]
    tokens = chunks * CHUNK
    operands = [arrived] + weights
    specs = [BLOCK] + [whole(a.shape) for a in weights]
    aliases = {}
    if earlier is not None:
        aliases = {len(operands): 0}
        operands.append(earlier)
        specs.append(pl.BlockSpec(memory_space=pl.ANY))
    return pl.pallas_call(
        grid_kernel,
        grid=(chunks,),
        in_specs=specs,
        out_specs=pl.BlockSpec((32, 1, 48, 128), lambda k: (0, base + k, 0, 0)),
        out_shape=jax.ShapeDtypeStruct((32, total, 48, 128), BF16),
        scratch_shapes=[pltpu.VMEM((CHUNK, 128), F32), pltpu.VMEM((CHUNK, 128), F32)]
        + ATTEND_SCRATCH
        + [pltpu.VMEM((TOKENS, HEADS * TOKENS), F32), pltpu.VMEM((HEADS, 16, 128), F32)],
        input_output_aliases=aliases,
        compiler_params=vm(48),
        cost_estimate=pl.CostEstimate(
            flops=tokens * 1000000, bytes_accessed=tokens * 800, transcendentals=tokens * 400
        ),
        name="grid",
    )(*operands)


def call_last(returned, w_in, w_back):
    chunks = returned.shape[1]
    tokens = chunks * CHUNK
    return pl.pallas_call(
        last_kernel,
        grid=(chunks,),
        in_specs=[BLOCK, whole(w_in.shape), whole(w_back.shape)],
        out_specs=pl.BlockSpec((ROWS_CHUNK, D, COLS), lambda k: (lax.rem(k + 1, chunks), 0, 0)),
        out_shape=jax.ShapeDtypeStruct((chunks * ROWS_CHUNK, D, COLS), BF16),
        scratch_shapes=[pltpu.VMEM((HID, D), BF16)],
        compiler_params=vm(48),
        cost_estimate=pl.CostEstimate(
            flops=tokens * 1000000, bytes_accessed=tokens * 800, transcendentals=tokens * 800
        ),
        name="last",
    )(returned, w_in, w_back)


def shift(x, axis, count, step):
    if step > 0:
        pairs = [(i, i + 1) for i in range(count - 1)]
    else:
        pairs = [(i + 1, i) for i in range(count - 1)]
    return lax.ppermute(x, axis, pairs)


ROW_AXES = ("y", "zh", "zl", "xl")
COL_AXES = ("xh", "core")
GROUP = ("y", "zh", "xh", "core")


def body(
    image, w_expand, dw_kernel, w_project, block_qkv, block_out, block_bias, mlp_in, mlp_out,
    grid_qkv, grid_out, grid_bias, mlp2_in, mlp2_out,
):
    edges = call_edge(image)
    here = lax.axis_index(COL_AXES)
    place = lax.broadcasted_iota(jnp.int32, (4, 1, 1), 0)
    none = jnp.zeros((), BF16)
    out = jnp.where(place == here + 1, edges[1][None], none)
    out = jnp.where(place == here - 1, edges[0][None], out)
    got = lax.all_to_all(out, COL_AXES, 0, 0, tiled=True)
    left = jnp.sum(jnp.where(place == here - 1, got, none), axis=0)
    right = jnp.sum(jnp.where(place == here + 1, got, none), axis=0)
    down, up = call_pack(image, left, right)
    top = shift(down, ROW_AXES, 32, 1)
    bottom = shift(up, ROW_AXES, 32, -1)
    weights = [
        w_expand, dw_kernel, w_project, block_qkv, block_out, block_bias, mlp_in, mlp_out
    ]
    inner = call_first(False, image, [down, up, left, right], weights)
    inner, top, bottom = lax.optimization_barrier((inner, top, bottom))
    one = lax.all_to_all(inner, GROUP, 0, 0, tiled=True)
    outer = call_first(True, image, [top, bottom, left, right], weights)
    two = lax.all_to_all(outer, GROUP, 0, 0, tiled=True)
    weights = [grid_qkv, grid_out, grid_bias]
    mixed = call_grid(0, 4, one, weights, None)
    mixed = call_grid(2, 4, two, weights, mixed)
    back = lax.all_to_all(mixed, GROUP, 0, 0, tiled=True)
    return call_last(back, mlp2_in, mlp2_out)


def solution(mesh):
    names = ("y", "zh", "zl", "xl", "xh", "core")
    fine = Mesh(mesh.devices.reshape(4, 2, 2, 2, 2, 2), names)
    spec = P(ROW_AXES, None, COL_AXES)
    return jax.shard_map(
        body, mesh=fine, in_specs=(spec,) + (P(),) * 13, out_specs=spec, check_vma=False
    )
```

```python
import functools
import math

import jax
import jax.numpy as jnp
from jax import lax
from jax.experimental import pallas as pl
from jax.experimental.pallas import tpu as pltpu
from jax.sharding import Mesh, PartitionSpec as P

WIN = 8
D = 192
HID = 768
HEADS = 6
SIZE = 32
COLS = 128
TOKENS = 64
CHUNK = 1024
ROWS_CHUNK = 8
TILES = 16
LAG = 3
LOG2E = 1.4426950408889634
F32 = jnp.float32
BF16 = jnp.bfloat16
NN = (((1,), (0,)), ((), ()))
NT = (((1,), (1,)), ((), ()))
TN = (((0,), (0,)), ((), ()))
C0 = math.sqrt(2.0 / math.pi)
C1 = 0.044715 * C0


def dot(a, b, dims=NN):
    return lax.dot_general(a, b, dims, preferred_element_type=F32)


def gelu(x):
    x = x.astype(BF16)
    inner = x * (BF16(C0) + BF16(C1) * (x * x))
    half = BF16(0.5) * x
    return half + half * jnp.tanh(inner)


def norm(s):
    centre = s - jnp.mean(s, axis=0, keepdims=True)
    spread = jnp.mean(centre * centre, axis=0, keepdims=True)
    return (centre * lax.rsqrt(spread + 1e-05)).astype(BF16)


def mlp(s, w_in_t, w_out):
    return s + dot(w_out, gelu(dot(w_in_t, norm(s))))


def softmax_keys(scores):
    top = jnp.max(scores, axis=0, keepdims=True)
    weights = jnp.exp2(scores - top)
    total = jnp.sum(weights, axis=0, keepdims=True)
    return (weights * (1.0 / total)).astype(BF16)


def attend(s, wq_t, wk, wv_t, w_out_t, bias):
    n = norm(s)
    q = dot(wq_t, n) * (SIZE**-0.5 * LOG2E)
    v = dot(wv_t, n).astype(BF16)
    k = dot(n, wk, TN).astype(BF16)
    left = lax.broadcasted_iota(jnp.int32, (1, 128), 1) < TOKENS
    keep = (lax.broadcasted_iota(jnp.int32, (TOKENS, 1), 0) < SIZE) == left
    zero = jnp.zeros((TOKENS, 128), BF16)
    tiles = s.shape[1] // 128
    ready = {}
    mixed = []

    def score(t):
        here = q[:, 128 * t : 128 * t + 128]
        swapped = pltpu.roll(here, TOKENS, 1).astype(BF16)
        here = here.astype(BF16)
        got = []
        for g in range(2):
            both = jnp.where(left, here, swapped) if g == 0 else jnp.where(left, swapped, here)
            keys = k[(2 * t + g) * TOKENS : (2 * t + g + 1) * TOKENS]
            b = [jnp.where(keep, both[64 * p : 64 * p + 64], zero) for p in range(3)]
            four = jnp.concatenate(
                [jnp.concatenate([b[0], zero], axis=1), jnp.concatenate([zero, b[1]], axis=1)],
                axis=0,
            )
            first = softmax_keys(dot(keys[:, :128], four) + bias[:, :256])
            last = softmax_keys(dot(keys[:, 128:], b[2]) + bias[:, 256:])
            got.append((first[:, :128], first[:, 128:], last))
        ready[t] = got

    def mix(t):
        got = ready.pop(t)
        values = v[:, 128 * t : 128 * t + 128]
        rows = []
        for p in range(3):
            pair = jnp.concatenate(
                [
                    jnp.concatenate([got[0][p], zero], axis=1),
                    jnp.concatenate([zero, got[1][p]], axis=1),
                ],
                axis=0,
            )
            out = dot(values[64 * p : 64 * p + 64], pair)
            a, b = out[:, :128], out[:, 128:]
            rows.append(jnp.where(left, a[:SIZE], pltpu.roll(b[:SIZE], TOKENS, 1)))
            rows.append(jnp.where(left, pltpu.roll(a[SIZE:], TOKENS, 1), b[SIZE:]))
        mixed.append(jnp.concatenate(rows, axis=0).astype(BF16))

    for t in range(tiles + LAG):
        if t < tiles:
            score(t)
        if t >= LAG:
            mix(t - LAG)
    return s + dot(w_out_t, jnp.concatenate(mixed, axis=1))


def bias_rows(table, padded, bias):
    lane = lax.broadcasted_iota(jnp.int32, (16, 128), 1)
    line = lax.broadcasted_iota(jnp.int32, (16, 128), 0)
    spread = jnp.where(lane // WIN == line, 1.0, 0.0)
    left = lax.broadcasted_iota(jnp.int32, (WIN, 128), 1) < TOKENS
    padded[...] = jnp.zeros_like(padded)
    heads = []
    for h in range(HEADS):
        padded[h, 0:15, 0:15] = table[h]
        cells = lax.dot_general(
            padded[h][:, :16], spread, TN, precision=lax.Precision.HIGHEST,
            preferred_element_type=F32,
        )
        rows = [
            jnp.sum(jnp.where(line == 7 - v + lane % WIN, cells, 0.0), axis=0, keepdims=True)
            for v in range(WIN)
        ]
        heads.append(jnp.concatenate(rows, axis=0))
    for u in range(WIN):
        for p in range(3):
            start = (7 - u) * WIN
            even = pltpu.roll(heads[2 * p], (128 - start) % 128, 1)
            odd = pltpu.roll(heads[2 * p + 1], (64 - start) % 128, 1)
            bias[u * WIN : (u + 1) * WIN, 128 * p : 128 * p + 128] = (
                jnp.where(left, even, odd) * LOG2E
            )


def prepare(w_qkv, w_out, table, wq_t, wk, wv_t, w_out_t, bias, padded):
    wq_t[...] = w_qkv[:, 0:D].T
    wk[...] = w_qkv[:, D : 2 * D]
    wv_t[...] = w_qkv[:, 2 * D : 3 * D].T
    w_out_t[...] = w_out[...].T
    bias_rows(table, padded, bias)


def gather_groups(lo, hi):
    parts = []
    for g in range(TILES):
        at = pl.ds(g, TOKENS, stride=TILES)
        parts.append(jnp.concatenate([lo[at, :], hi[at, :][:, :64]], axis=1))
    return jnp.concatenate(parts, axis=0).T


def first_kernel(
    edge, image, before, after, top, bottom, left, right,
    w_expand, taps, w_project, w_qkv, w_out, table, w_in, w_back,
    out, expanded, mobile, tokens, lo, hi, place, wq_t, wk, wv_t, w_out_t, w_in_t, bias, padded,
    dw, side,
):
    step = pl.program_id(0)
    line = lax.broadcasted_iota(jnp.int32, (16, HID), 0)

    def laid(x):
        return dot(place[...], x, NT).astype(BF16)

    def expand(x, sides, rows):
        cells = gelu(dot(x, w_expand[...])).astype(F32)
        for i, r in enumerate(rows):
            e = cells[COLS * i : COLS * (i + 1)]
            expanded[r, 16:144, :] = e
            prev = pltpu.roll(e[112:128], 1, 0)
            expanded[r, 0:16, :] = jnp.where(line == 0, sides[0][r : r + 1], prev)
            follow = pltpu.roll(e[0:16], 15, 0)
            expanded[r, 144:160, :] = jnp.where(line == 15, sides[1][r : r + 1], follow)

    @pl.when(step == 0)
    def _():
        for i in range(3):
            dw[3 * i : 3 * i + 3, :] = taps[i].astype(F32)
        for i, halo in enumerate((left, right)):
            side[i, 8:40, :] = gelu(dot(halo[...], w_expand[...])).astype(F32)
            if edge:
                for j, message in enumerate((top, bottom)):
                    pair = message[D + 32 * i : D + 32 * i + 32, :]
                    corner = jnp.concatenate([pair[0:16], pair[16:32, 0:64]], axis=1)
                    ends = gelu(dot(corner, w_expand[...])).astype(F32)
                    side[i, 40 * j : 40 * j + 8, :] = jnp.broadcast_to(ends[0:1], (8, HID))
        prepare(w_qkv, w_out, table, wq_t, wk, wv_t, w_out_t, bias, padded)
        w_in_t[...] = w_in[...].T
        row = lax.broadcasted_iota(jnp.int32, (COLS, COLS), 0)
        col = lax.broadcasted_iota(jnp.int32, (COLS, COLS), 1)
        place[...] = jnp.where(col == (row % 16) * 8 + row // 16, 1.0, 0.0).astype(BF16)

    order = (step + 1) if not edge else jnp.where(step == 0, 3, 0)
    start = pl.multiple_of(order * ROWS_CHUNK, 8)
    sides = [side[i, pl.ds(start, 24), :][7:23] for i in range(2)]

    def begin():
        above = before[0]
        if edge:
            above = jnp.where(step == 0, above, top[0:D, :])
        pair = jnp.concatenate([laid(above), laid(image[0])], axis=0)
        tokens[0:COLS, :] = pair[COLS:]
        expand(pair, sides, (0, 1))

    below = after[0]
    if edge:
        below = jnp.where(step == 0, bottom[0:D, :], below)
        begin()
    else:
        pl.when(step == 0)(begin)

        @pl.when(step > 0)
        def _():
            tokens[0:COLS, :] = tokens[8 * COLS : 9 * COLS, :]
            expanded[0:2] = expanded[8:10]

    for r in range(1, ROWS_CHUNK):
        tokens[COLS * r : COLS * (r + 1), :] = laid(image[r])
    tokens[COLS * 8 : COLS * 9, :] = laid(below)
    for half in range(2):
        x = tokens[COLS * (1 + 4 * half) : COLS * (5 + 4 * half), :]
        expand(x, sides, range(2 + 4 * half, 6 + 4 * half))

    for r in range(ROWS_CHUNK):
        for block in range(HID // 128):
            lanes = slice(block * 128, (block + 1) * 128)
            conv = None
            for i in range(3):
                for k in range(3):
                    term = expanded[r + i, 16 * k : 16 * k + COLS, lanes] * dw[
                        3 * i + k : 3 * i + k + 1, lanes
                    ]
                    conv = term if conv is None else conv + term
            mobile[COLS * r : COLS * (r + 1), lanes] = gelu(conv)

    s = tokens[0:CHUNK, :].astype(F32) + dot(mobile[...], w_project[...], NT)
    lo[...] = s[:, :128]
    hi[:, :64] = s[:, 128:]
    s = gather_groups(lo, hi)
    s = attend(s, wq_t[...], wk[...], wv_t[...], w_out_t[...], bias)
    s = mlp(s, w_in_t[...], w_back[...]).T.reshape(TILES, WIN, WIN, D)
    for r in range(ROWS_CHUNK):
        rows = s[:, r].reshape(2, 4, 16, D)
        at = slice(4 * r, 4 * r + 4)
        out[at, 0, 0:16, :] = rows[0, :, :, 0:128].astype(BF16)
        out[at, 0, 16:32, :] = rows[1, :, :, 0:128].astype(BF16)
        out[at, 0, 32:48, :] = jnp.concatenate(
            [rows[0, :, :, 128:], rows[1, :, :, 128:]], axis=-1
        ).astype(BF16)


def grid_kernel(inp, w_qkv, w_out, table, *rest):
    out, lo, hi, wq_t, wk, wv_t, w_out_t, bias, padded = rest[-9:]

    @pl.when(pl.program_id(0) == 0)
    def _():
        prepare(w_qkv, w_out, table, wq_t, wk, wv_t, w_out_t, bias, padded)

    for src in range(32):
        lo[32 * src : 32 * src + 32, :] = inp[src, 0, 0:32, :].astype(F32)
        both = inp[src, 0, 32:48, :].astype(F32)
        hi[32 * src : 32 * src + 16, :] = both
        hi[32 * src + 16 : 32 * src + 32, :] = pltpu.roll(both, 64, 1)
    s = gather_groups(lo, hi)
    s = attend(s, wq_t[...], wk[...], wv_t[...], w_out_t[...], bias).T
    for g in range(TILES):
        at = pl.ds(g, TOKENS, stride=TILES)
        rows = s[g * TOKENS : (g + 1) * TOKENS]
        lo[at, :] = rows[:, :128]
        hi[at, :] = jnp.concatenate([rows[:, 128:], rows[:, 128:]], axis=1)
    left = lax.broadcasted_iota(jnp.int32, (16, 128), 1) < 64
    for src in range(32):
        out[src, 0, 0:32, :] = lo[32 * src : 32 * src + 32, :].astype(BF16)
        out[src, 0, 32:48, :] = jnp.where(
            left, hi[32 * src : 32 * src + 16, :], hi[32 * src + 16 : 32 * src + 32, :]
        ).astype(BF16)


def last_kernel(inp, w_in, w_back, out, w_in_t):
    @pl.when(pl.program_id(0) == 0)
    def _():
        w_in_t[...] = w_in[...].T

    rows = []
    for r in range(ROWS_CHUNK):
        got = inp[4 * r : 4 * r + 4, 0]
        both = got[:, 32:48].reshape(64, 128)
        for i in range(2):
            low = got[:, 16 * i : 16 * i + 16].reshape(64, 128)
            rows.append(jnp.concatenate([low, both[:, 64 * i : 64 * i + 64]], axis=1))
    s = jnp.concatenate(rows, axis=0).T.astype(F32)
    s = mlp(s, w_in_t[...], w_back[...]).astype(BF16)
    for r in range(ROWS_CHUNK):
        out[r] = s[:, COLS * r : COLS * (r + 1)]


def pack_kernel(lowest, highest, left, right, down, up):
    for r, cells, out in ((left.shape[0] - 1, lowest, down), (0, highest, up)):
        out[0:D, :] = cells[0]
        for i, halo in enumerate((left, right)):
            cell = halo[r : r + 1, :].astype(F32)
            high = jnp.concatenate([cell[:, 128:], cell[:, 128:]], axis=1)
            at = D + 32 * i
            out[at : at + 16, :] = jnp.broadcast_to(cell[:, :128], (16, 128)).astype(BF16)
            out[at + 16 : at + 32, :] = jnp.broadcast_to(high, (16, 128)).astype(BF16)


def edge_kernel(image, out):
    rows = image.shape[0]
    row = lax.broadcasted_iota(jnp.int32, (2 * rows, COLS * rows), 0)
    col = lax.broadcasted_iota(jnp.int32, (2 * rows, COLS * rows), 1)
    wanted = jnp.where(row < rows, row * COLS, (row - rows) * COLS + COLS - 1)
    pick = jnp.where(col == wanted, 1.0, 0.0).astype(BF16)
    cells = jnp.concatenate([image[r] for r in range(rows)], axis=1)
    got = dot(pick, cells, NT).astype(BF16)
    out[0] = got[:rows]
    out[1] = got[rows:]


def whole(shape):
    return pl.BlockSpec(shape, lambda k: (0,) * len(shape))


def vm(limit):
    return pltpu.CompilerParams(vmem_limit_bytes=limit << 20, dimension_semantics=("arbitrary",))


BLOCK = pl.BlockSpec((32, 1, 48, 128), lambda k: (0, k, 0, 0))
ATTEND_SCRATCH = [
    pltpu.VMEM((D, D), BF16),
    pltpu.VMEM((D, D), BF16),
    pltpu.VMEM((D, D), BF16),
    pltpu.VMEM((D, D), BF16),
]


def call_edge(image):
    rows = image.shape[0]
    return pl.pallas_call(
        edge_kernel,
        out_shape=jax.ShapeDtypeStruct((2, rows, D), BF16),
        compiler_params=pltpu.CompilerParams(vmem_limit_bytes=32 << 20),
        cost_estimate=pl.CostEstimate(flops=4000000, bytes_accessed=1600000, transcendentals=0),
        name="edge",
    )(image)


def call_pack(image, left, right):
    shape = jax.ShapeDtypeStruct((D + 64, COLS), BF16)
    rows = image.shape[0]
    return pl.pallas_call(
        pack_kernel,
        grid=(1,),
        in_specs=[
            pl.BlockSpec((1, D, COLS), lambda k: (rows - 1, 0, 0)),
            pl.BlockSpec((1, D, COLS), lambda k: (0, 0, 0)),
            whole(left.shape),
            whole(right.shape),
        ],
        out_specs=(whole(shape.shape), whole(shape.shape)),
        out_shape=(shape, shape),
        compiler_params=pltpu.CompilerParams(vmem_limit_bytes=32 << 20),
        cost_estimate=pl.CostEstimate(flops=40000, bytes_accessed=200000, transcendentals=0),
        name="pack",
    )(image, image, left, right)


def call_first(edge, image, halos, weights):
    chunks = 2
    total = image.shape[0]

    def chunk(k):
        return 3 - 3 * k if edge else 1 + k

    rows = pl.BlockSpec((ROWS_CHUNK, D, COLS), lambda k: (chunk(k), 0, 0))
    before = pl.BlockSpec(
        (1, D, COLS), lambda k: (jnp.maximum(chunk(k) * ROWS_CHUNK - 1, 0), 0, 0)
    )
    after = pl.BlockSpec(
        (1, D, COLS), lambda k: (jnp.minimum((chunk(k) + 1) * ROWS_CHUNK, total - 1), 0, 0)
    )
    small = halos + weights
    tokens = chunks * CHUNK
    return pl.pallas_call(
        functools.partial(first_kernel, edge),
        grid=(chunks,),
        in_specs=[rows, before, after] + [whole(a.shape) for a in small],
        out_specs=BLOCK,
        out_shape=jax.ShapeDtypeStruct((32, chunks, 48, 128), BF16),
        scratch_shapes=[
            pltpu.VMEM((ROWS_CHUNK + 2, 160, HID), F32),
            pltpu.VMEM((CHUNK, HID), BF16),
            pltpu.VMEM((9 * COLS, D), BF16),
            pltpu.VMEM((CHUNK, 128), F32),
            pltpu.VMEM((CHUNK, 128), F32),
            pltpu.VMEM((COLS, COLS), BF16),
        ]
        + ATTEND_SCRATCH
        + [
            pltpu.VMEM((HID, D), BF16),
            pltpu.VMEM((TOKENS, HEADS * TOKENS), F32),
            pltpu.VMEM((HEADS, 16, 128), F32),
            pltpu.VMEM((9, HID), F32),
            pltpu.VMEM((2, 48, HID), F32),
        ],
        compiler_params=vm(60 if edge else 48),
        cost_estimate=pl.CostEstimate(
            flops=tokens * 2000000, bytes_accessed=tokens * 800, transcendentals=tokens * 2700
        ),
        name="first",
    )(image, image, image, *small)


def call_grid(base, total, arrived, weights, earlier):
    chunks = arrived.shape[1]
    tokens = chunks * CHUNK
    operands = [arrived] + weights
    specs = [BLOCK] + [whole(a.shape) for a in weights]
    aliases = {}
    if earlier is not None:
        aliases = {len(operands): 0}
        operands.append(earlier)
        specs.append(pl.BlockSpec(memory_space=pl.ANY))
    return pl.pallas_call(
        grid_kernel,
        grid=(chunks,),
        in_specs=specs,
        out_specs=pl.BlockSpec((32, 1, 48, 128), lambda k: (0, base + k, 0, 0)),
        out_shape=jax.ShapeDtypeStruct((32, total, 48, 128), BF16),
        scratch_shapes=[pltpu.VMEM((CHUNK, 128), F32), pltpu.VMEM((CHUNK, 128), F32)]
        + ATTEND_SCRATCH
        + [pltpu.VMEM((TOKENS, HEADS * TOKENS), F32), pltpu.VMEM((HEADS, 16, 128), F32)],
        input_output_aliases=aliases,
        compiler_params=vm(48),
        cost_estimate=pl.CostEstimate(
            flops=tokens * 1000000, bytes_accessed=tokens * 800, transcendentals=tokens * 400
        ),
        name="grid",
    )(*operands)


def call_last(returned, w_in, w_back):
    chunks = returned.shape[1]
    tokens = chunks * CHUNK
    return pl.pallas_call(
        last_kernel,
        grid=(chunks,),
        in_specs=[BLOCK, whole(w_in.shape), whole(w_back.shape)],
        out_specs=pl.BlockSpec((ROWS_CHUNK, D, COLS), lambda k: (lax.rem(k + 1, chunks), 0, 0)),
        out_shape=jax.ShapeDtypeStruct((chunks * ROWS_CHUNK, D, COLS), BF16),
        scratch_shapes=[pltpu.VMEM((HID, D), BF16)],
        compiler_params=vm(48),
        cost_estimate=pl.CostEstimate(
            flops=tokens * 1000000, bytes_accessed=tokens * 800, transcendentals=tokens * 800
        ),
        name="last",
    )(returned, w_in, w_back)


def shift(x, axis, count, step):
    if step > 0:
        pairs = [(i, i + 1) for i in range(count - 1)]
    else:
        pairs = [(i + 1, i) for i in range(count - 1)]
    return lax.ppermute(x, axis, pairs)


ROW_AXES = ("y", "zh", "zl", "xl")
COL_AXES = ("xh", "core")
GROUP = ("y", "zh", "xh", "core")


def body(
    image, w_expand, dw_kernel, w_project, block_qkv, block_out, block_bias, mlp_in, mlp_out,
    grid_qkv, grid_out, grid_bias, mlp2_in, mlp2_out,
):
    edges = call_edge(image)
    here = lax.axis_index(COL_AXES)
    place = lax.broadcasted_iota(jnp.int32, (4, 1, 1), 0)
    none = jnp.zeros((), BF16)
    out = jnp.where(place == here + 1, edges[1][None], none)
    out = jnp.where(place == here - 1, edges[0][None], out)
    got = lax.all_to_all(out, COL_AXES, 0, 0, tiled=True)
    left = jnp.sum(jnp.where(place == here - 1, got, none), axis=0)
    right = jnp.sum(jnp.where(place == here + 1, got, none), axis=0)
    down, up = call_pack(image, left, right)
    top = shift(down, ROW_AXES, 32, 1)
    bottom = shift(up, ROW_AXES, 32, -1)
    weights = [
        w_expand, dw_kernel, w_project, block_qkv, block_out, block_bias, mlp_in, mlp_out
    ]
    inner = call_first(False, image, [down, up, left, right], weights)
    inner, top, bottom = lax.optimization_barrier((inner, top, bottom))
    one = lax.all_to_all(inner, GROUP, 0, 0, tiled=True)
    outer = call_first(True, image, [top, bottom, left, right], weights)
    two = lax.all_to_all(outer, GROUP, 0, 0, tiled=True)
    weights = [grid_qkv, grid_out, grid_bias]
    mixed = call_grid(0, 4, one, weights, None)
    mixed = call_grid(2, 4, two, weights, mixed)
    back = lax.all_to_all(mixed, GROUP, 0, 0, tiled=True)
    return call_last(back, mlp2_in, mlp2_out)


def solution(mesh):
    names = ("y", "zh", "zl", "xl", "xh", "core")
    fine = Mesh(mesh.devices.reshape(4, 2, 2, 2, 2, 2), names)
    spec = P(ROW_AXES, None, COL_AXES)
    return jax.shard_map(
        body, mesh=fine, in_specs=(spec,) + (P(),) * 13, out_specs=spec, check_vma=False
    )
```
